256 devices in a mesh: ctx: 128 (over z, y, x), head: 2 (over core).
Axes of the slice: x: 4, y: 4, z: 8, core: 2. Of those that a mesh axis runs over, the one named last changes fastest.
Arguments:
- queries: bfloat16 [16384, 2048], P('ctx', 'head'), may hold values from -6 to 6
- keys: bfloat16 [16384, 128], P('ctx'), may hold values from -6 to 6
- values: bfloat16 [16384, 128], P('ctx'), may hold values from -6 to 6
- d_out: bfloat16 [16384, 2048], P('ctx', 'head'), may hold values from -6 to 6
- doc_starts: int32 [16], replicated, may hold values from 0 to 15872, as said below
- assign: int32 [256], replicated, may hold values from 0 to 255, as said below
Outputs:
- attn_out: bfloat16 [16384, 2048], P('ctx', 'head')
- d_query: bfloat16 [16384, 2048], P('ctx', 'head')
- d_key: bfloat16 [16384, 128], P('ctx')
- d_value: bfloat16 [16384, 128], P('ctx')
The draws below stay inside these ranges and needn't reach their ends.
Inputs may be any that keep to these rules, and one draw needn't show every extreme that they name: `doc_starts`: increasing multiples of 512 beginning with 0; document i runs from entry i to the next entry, the last one to 16384. A permutation: storage span c of every sequence array holds the positions assign[c] * 64 to assign[c] * 64 + 63.
All inputs are finite; a program needn't handle non-finite values.
Results may differ from the reference program's by a relative error of at most 0.035.
Values may be sent and summed in bfloat16 or wider, within the bound.
A program may use at most 128 MiB of HBM per device.

```python
import math
import jax
import jax.numpy as jnp
from jax import lax

HD = 128
QH = 16
KEY_BLOCK = 512
UNIT = 512
SPAN = 64
TOKENS = 16384
NCHUNK = 256
NDOC = 16


def start_table(key):
    grid_points = TOKENS // UNIT
    if NDOC > 1:
        cut_points = jax.random.permutation(jax.random.fold_in(key, 11), grid_points - 2) + 1
        chosen = jnp.sort(cut_points[:NDOC - 2]).astype(jnp.int32)
        last_cut = jnp.full((1,), grid_points - 1, jnp.int32)
        return (jnp.concatenate([jnp.zeros((1,), jnp.int32), chosen, last_cut]) * UNIT).astype(jnp.int32)
    return jnp.zeros((1,), jnp.int32)


def span_table(key):
    return jax.random.permutation(jax.random.fold_in(key, 12), NCHUNK).astype(jnp.int32)


def draw_doc_starts(key, part):
    shared = start_table(key)
    return shared


def draw_assign(key, part):
    shared = span_table(key)
    return shared


def draw_queries(key, part):
    key = jax.random.fold_in(key, 3)
    drawn = jnp.clip(jax.random.normal(key, (TOKENS, QH * HD), jnp.float32), -6.0, 6.0)
    return drawn.astype(jnp.bfloat16)


def draw_keys(key, part):
    key = jax.random.fold_in(key, 4)
    drawn = jnp.clip(jax.random.normal(key, (TOKENS, HD), jnp.float32), -6.0, 6.0)
    return drawn.astype(jnp.bfloat16)


def shard_levels(key, shape, pieces, least, top_value):
    def one(dim, shards_of):
        heights = jax.random.uniform(jax.random.fold_in(jax.random.fold_in(key, 6), dim), (shards_of,), jnp.float32, least / len(pieces), top_value / len(pieces))
        return jnp.repeat(jnp.exp(heights), shape[dim] // shards_of).reshape((-1,) + (1,) * (len(shape) - dim - 1))

    gain = one(*pieces[0])
    for cut in pieces[1:]:
        gain = gain * one(*cut)
    return gain


def bell_draw(stream_key, shape, scale, most, pieces=(), kind=jnp.bfloat16):
    level = shard_levels(stream_key, shape, pieces, -0.22, 0.18) if pieces else 1.0
    values = jax.random.normal(stream_key, shape, jnp.float32) * scale * level
    return jnp.minimum(jnp.maximum(values, -most), most).astype(kind)


def setup_inputs(seed: int = 0) -> dict:
    splits = jax.random.split(jax.random.key(seed), 7)
    queries = draw_queries(jax.random.fold_in(splits[6], 71), 0)
    keys = draw_keys(jax.random.fold_in(splits[6], 71), 0)
    values = bell_draw(splits[2], (TOKENS, HD), 1.0, 6.0, ((0, 128),))
    d_out = bell_draw(splits[3], (TOKENS, QH * HD), 1.0, 6.0, ((0, 128), (1, 2)))
    doc_starts = draw_doc_starts(jax.random.fold_in(splits[6], 71), 0)
    assign = draw_assign(jax.random.fold_in(splits[6], 71), 0)
    return {"queries": queries, "keys": keys, "values": values, "d_out": d_out, "doc_starts": doc_starts, "assign": assign}


masked_value = -1e+30

def span_rows(assign):
    span_total = assign.shape[0]
    span_order = jnp.zeros((span_total,), jnp.int32).at[assign].set(jnp.arange(span_total, dtype=jnp.int32))
    positions = jnp.arange(TOKENS, dtype=jnp.int32)
    to_storage = span_order[positions // SPAN] * SPAN + positions % SPAN
    to_position = assign[positions // SPAN] * SPAN + positions % SPAN
    return (to_storage.astype(jnp.int32), to_position.astype(jnp.int32))

def reference(queries, keys, values, d_out, doc_starts, assign):
    to_storage, to_position = span_rows(assign)
    score_scale = 1.0 / math.sqrt(HD)
    q_all = jnp.take(queries, to_storage, axis=0).reshape(TOKENS, QH, HD)
    g_all = jnp.take(d_out, to_storage, axis=0).reshape(TOKENS, QH, HD)
    k_all = jnp.take(keys, to_storage, axis=0)
    v_all = jnp.take(values, to_storage, axis=0)
    positions = jnp.arange(TOKENS, dtype=jnp.int32)
    doc_first = lax.optimization_barrier(jnp.max(jnp.where(doc_starts[None, :] <= positions[:, None], doc_starts[None, :], 0), axis=1)).astype(jnp.int32)
    block_keys = jnp.arange(KEY_BLOCK, dtype=jnp.int32)
    block_count = TOKENS // KEY_BLOCK

    def query_block(block_index):
        start = (block_index * KEY_BLOCK).astype(jnp.int32)
        q_block = lax.dynamic_slice_in_dim(q_all, start, KEY_BLOCK, 0).astype(jnp.float32)
        g_block = lax.dynamic_slice_in_dim(g_all, start, KEY_BLOCK, 0).astype(jnp.float32)
        q_first = lax.dynamic_slice_in_dim(doc_first, start, KEY_BLOCK, 0)
        return (q_block, g_block, start + block_keys, q_first)

    def key_block(key_index):
        start = (key_index * KEY_BLOCK).astype(jnp.int32)
        k_tile = lax.dynamic_slice_in_dim(k_all, start, KEY_BLOCK, 0).astype(jnp.float32)
        v_tile = lax.dynamic_slice_in_dim(v_all, start, KEY_BLOCK, 0).astype(jnp.float32)
        return (k_tile, v_tile, start + block_keys)

    def score_tile(q_block, q_place, q_first, k_tile, key_place):
        scores = jnp.einsum('qhd,kd->qhk', q_block, k_tile) * score_scale
        allowed = (key_place[None, None, :] >= q_first[:, None, None]) & (key_place[None, None, :] <= q_place[:, None, None])
        return (scores, allowed)

    def probs_of(scores, allowed, log_total):
        rounded = jnp.where(allowed, jnp.exp(scores - log_total[:, :, None]), 0.0).astype(jnp.bfloat16)
        return lax.optimization_barrier(rounded).astype(jnp.float32)

    def grads_of(probs, g_block, v_tile, delta_rows):
        d_probs = jnp.einsum('qhd,kd->qhk', g_block, v_tile)
        rounded = (probs * (d_probs - delta_rows[:, :, None]) * score_scale).astype(jnp.bfloat16)
        return lax.optimization_barrier(rounded).astype(jnp.float32)

    def forward(block_index):
        q_block, g_block, q_place, q_first = query_block(block_index)
        first_block = (q_first[0] // KEY_BLOCK).astype(jnp.int32)
        last_block = (block_index + 1).astype(jnp.int32)

        def stats_step(key_index, state_now):
            running_max, running_sum = state_now
            k_tile, v_tile, key_place = key_block(key_index)
            scores, allowed = score_tile(q_block, q_place, q_first, k_tile, key_place)
            scores = jnp.where(allowed, scores, masked_value)
            new_max = jnp.maximum(running_max, lax.optimization_barrier(jnp.max(scores, axis=2)))
            weights = jnp.where(allowed, jnp.exp(scores - new_max[:, :, None]), 0.0)
            return (new_max, running_sum * jnp.exp(running_max - new_max) + lax.optimization_barrier(jnp.sum(weights, axis=2)))
        start_state = (jnp.full((KEY_BLOCK, QH), masked_value, jnp.float32), jnp.zeros((KEY_BLOCK, QH), jnp.float32))
        running_max, running_sum = lax.fori_loop(first_block, last_block, stats_step, start_state)
        log_total = running_max + jnp.log(running_sum)

        def output_step(key_index, attn_acc):
            k_tile, v_tile, key_place = key_block(key_index)
            scores, allowed = score_tile(q_block, q_place, q_first, k_tile, key_place)
            probs = probs_of(scores, allowed, log_total)
            return attn_acc + jnp.einsum('qhk,kd->qhd', probs, v_tile)
        attn_acc = lax.fori_loop(first_block, last_block, output_step, jnp.zeros((KEY_BLOCK, QH, HD), jnp.float32))
        attn_rows = attn_acc.astype(jnp.bfloat16)
        delta_rows = lax.optimization_barrier(jnp.sum(g_block * attn_rows.astype(jnp.float32), axis=2))

        def query_step(key_index, query_acc):
            k_tile, v_tile, key_place = key_block(key_index)
            scores, allowed = score_tile(q_block, q_place, q_first, k_tile, key_place)
            probs = probs_of(scores, allowed, log_total)
            d_scores = grads_of(probs, g_block, v_tile, delta_rows)
            return query_acc + jnp.einsum('qhk,kd->qhd', d_scores, k_tile)
        query_acc = lax.fori_loop(first_block, last_block, query_step, jnp.zeros((KEY_BLOCK, QH, HD), jnp.float32))
        return (attn_rows, query_acc.astype(jnp.bfloat16), log_total, delta_rows)
    attn_rows, query_rows, log_all, delta_all = lax.map(forward, jnp.arange(block_count, dtype=jnp.int32))
    block_firsts = doc_first[::KEY_BLOCK]

    def backward(key_index):
        k_tile, v_tile, key_place = key_block(key_index)
        last_block = jnp.sum((block_firsts < (key_index + 1) * KEY_BLOCK).astype(jnp.int32)).astype(jnp.int32)

        def key_step(block_index, state_now):
            key_acc, value_acc = state_now
            q_block, g_block, q_place, q_first = query_block(block_index)
            log_total = log_all[block_index]
            delta_rows = delta_all[block_index]
            scores, allowed = score_tile(q_block, q_place, q_first, k_tile, key_place)
            probs = probs_of(scores, allowed, log_total)
            d_scores = grads_of(probs, g_block, v_tile, delta_rows)
            key_acc = key_acc + jnp.einsum('qhk,qhd->kd', d_scores, q_block)
            value_acc = value_acc + jnp.einsum('qhk,qhd->kd', probs, g_block)
            return (key_acc, value_acc)
        start_state = (jnp.zeros((KEY_BLOCK, HD), jnp.float32), jnp.zeros((KEY_BLOCK, HD), jnp.float32))
        key_acc, value_acc = lax.fori_loop(key_index.astype(jnp.int32), last_block, key_step, start_state)
        return (key_acc.astype(jnp.bfloat16), value_acc.astype(jnp.bfloat16))
    key_rows, value_rows = lax.map(backward, jnp.arange(block_count, dtype=jnp.int32))
    attn_out = jnp.take(attn_rows.reshape(TOKENS, QH * HD), to_position, axis=0)
    d_query = jnp.take(query_rows.reshape(TOKENS, QH * HD), to_position, axis=0)
    d_key = jnp.take(key_rows.reshape(TOKENS, HD), to_position, axis=0)
    d_value = jnp.take(value_rows.reshape(TOKENS, HD), to_position, axis=0)
    return (attn_out, d_query, d_key, d_value)
```

```python
import functools
import math

import jax
import jax.numpy as jnp
from jax import lax
from jax.experimental import pallas as pl
from jax.experimental.pallas import tpu as pltpu
from jax.sharding import PartitionSpec as P

HD = 128
SPAN = 64
BLOCK = 512
UNIT = 512
MESH = pl.DeviceIdType.MESH
AXES = ("z", "y", "x")
SIZES = {"z": 8, "y": 4, "x": 4}
PARTS = (
    (0, 32, ("y", "x", "z")),
    (32, 48, ("z", "y", "x")),
    (80, 48, ("z", "x", "y")),
)
VMEM_BYTES = 60 * 1024 * 1024


def my_place():
    me = lax.axis_index("ctx")
    nx, ny = SIZES["x"], SIZES["y"]
    pos = {"x": lax.rem(me, nx), "y": lax.rem(me // nx, ny), "z": me // (nx * ny)}
    return pos, me, lax.axis_index("head")


def wrapped(value, size):
    return lax.rem(value + 2 * size, size)


def ring_peer(pos, core, axis, step):
    there = dict(pos)
    there[axis] = wrapped(pos[axis] + step, SIZES[axis])
    return ((there["z"] * SIZES["y"] + there["y"]) * SIZES["x"] + there["x"], core)


def greet(pos, me, core):
    barrier = pltpu.get_barrier_semaphore()
    for axis in AXES:
        for step in (1, -1):
            pl.semaphore_signal(
                barrier, inc=1, device_id=ring_peer(pos, core, axis, step), device_id_type=MESH
            )
    pl.semaphore_signal(barrier, inc=1, device_id=(me, 1 - core), device_id_type=MESH)
    pl.semaphore_wait(barrier, 2 * len(AXES) + 1)


def row_half(first, count, side):
    low = count // 32 * 16 if count % 32 == 0 else (count // 32 + 1) * 16
    return (first, low) if side == 0 else (first + low, count - low)


def axis_half(axis, side):
    half = SIZES[axis] // 2
    return (side * half, half)


def spans(sel):
    return tuple(pl.ds(first, count) for first, count in sel)


def gather_view(pos, part, stage, index, half):
    first, count, order = PARTS[part]
    sel = {}
    for rank, axis in enumerate(order):
        if rank < stage:
            sel[axis] = (0, SIZES[axis])
        elif rank == stage:
            sel[axis] = (index, 1)
        else:
            sel[axis] = (pos[axis], 1)
    rows = (first, count)
    if half is not None:
        if stage == 0:
            rows = row_half(first, count, half)
        else:
            sel[order[0]] = axis_half(order[0], half)
    return spans([sel[axis] for axis in AXES] + [rows])


def ring_steps(order):
    return [(stage, step) for stage, axis in enumerate(order) for step in range(1, SIZES[axis] // 2 + 1)]


def gather_kernel(kv_ref, all_ref, send, recv, side_send, side_recv, local_sem):
    pos, me, core = my_place()
    greet(pos, me, core)
    mine = pltpu.make_async_copy(
        kv_ref, all_ref.at[:, pl.ds(pos["z"], 1), pl.ds(pos["y"], 1), pl.ds(pos["x"], 1)], local_sem
    )
    mine.start()

    def copy(part, stage, step, way, arriving):
        order = PARTS[part][2]
        axis = order[stage]
        toward = 1 - 2 * way
        index = wrapped(pos[axis] - toward * (step if arriving else step - 1), SIZES[axis])
        half = way if step == SIZES[axis] // 2 else None
        view = gather_view(pos, part, stage, index, half)
        src = all_ref.at[(core, *view)]
        if not arriving and stage == 0 and step == 1:
            src = kv_ref.at[(core, pl.ds(0, 1), pl.ds(0, 1), pl.ds(0, 1), view[3])]
        return pltpu.make_async_remote_copy(
            src_ref=src,
            dst_ref=all_ref.at[(core, *view)],
            send_sem=send.at[part, stage, step - 1, way],
            recv_sem=recv.at[part, stage, step - 1, way],
            device_id=ring_peer(pos, core, axis, toward),
            device_id_type=MESH,
        )

    def side_copy(part, stage, step, way, owner):
        axis = PARTS[part][2][stage]
        toward = 1 - 2 * way
        index = wrapped(pos[axis] - toward * step, SIZES[axis])
        half = way if step == SIZES[axis] // 2 else None
        view = gather_view(pos, part, stage, index, half)
        return pltpu.make_async_remote_copy(
            src_ref=all_ref.at[(owner, *view)],
            dst_ref=all_ref.at[(owner, *view)],
            send_sem=side_send.at[part, stage, step - 1, way],
            recv_sem=side_recv.at[part, stage, step - 1, way],
            device_id=(me, 1 - core),
            device_id_type=MESH,
        )

    plans = [ring_steps(order) for _, _, order in PARTS]
    longest = max(len(plan) for plan in plans)
    for slot in range(longest + 1):
        for part, plan in enumerate(plans):
            if slot > len(plan):
                continue
            if slot > 0:
                for way in (0, 1):
                    copy(part, *plan[slot - 1], way, True).wait_recv()
            if slot < len(plan):
                for way in (0, 1):
                    copy(part, *plan[slot], way, False).start()
            if slot > 0:
                for way in (0, 1):
                    side_copy(part, *plan[slot - 1], way, core).start()
        if slot == 0:
            mine.wait()
    for part, plan in enumerate(plans):
        for stage, step in plan:
            for way in (0, 1):
                copy(part, stage, step, way, False).wait_send()
                side_copy(part, stage, step, way, core).wait_send()
                side_copy(part, stage, step, way, 1 - core).wait_recv()


def gather_all(kv):
    dims = tuple(SIZES[axis] for axis in AXES)
    sems = pltpu.SemaphoreType.DMA((len(PARTS), 3, 4, 2))
    return pl.pallas_call(
        gather_kernel,
        out_shape=jax.ShapeDtypeStruct((2, *dims, 2 * SPAN, HD), jnp.bfloat16),
        in_specs=[pl.BlockSpec(memory_space=pl.ANY)],
        out_specs=pl.BlockSpec(memory_space=pl.ANY),
        scratch_shapes=[sems, sems, sems, sems, pltpu.SemaphoreType.DMA],
        compiler_params=pltpu.CompilerParams(collective_id=0, has_side_effects=True),
    )(kv)


def sum_views(pos, part, stage, index, half):
    first, count, gather_order = PARTS[part]
    order = gather_order[::-1]
    held, landed = {}, {}
    for rank, axis in enumerate(order):
        if rank < stage:
            held[axis], landed[axis] = (pos[axis], 1), (0, 1)
        elif rank == stage:
            held[axis] = landed[axis] = (index, 1)
        else:
            held[axis] = landed[axis] = (0, SIZES[axis])
    rows = (0, count)
    if half is not None:
        if stage == 2:
            rows = row_half(0, count, half)
        else:
            held[order[2]] = landed[order[2]] = axis_half(order[2], half)
    return (
        [held[axis] for axis in AXES] + [(first + rows[0], rows[1])],
        [landed[axis] for axis in AXES] + [rows],
    )


def landing_shape(part, stage):
    _, count, gather_order = PARTS[part]
    order = gather_order[::-1]
    dims = tuple(1 if order.index(axis) < stage else SIZES[axis] for axis in AXES)
    return (2, *dims, count, HD)


def each_chunk(counts, body):
    widest = max(range(3), key=lambda i: counts[i])
    others = [i for i in range(3) if i != widest]

    def step(at, carry):
        for a in range(counts[others[0]]):
            for b in range(counts[others[1]]):
                place = [None] * 3
                place[widest], place[others[0]], place[others[1]] = at, a, b
                body(place)
        return carry

    if counts[widest] == 1:
        step(0, 0)
    else:
        lax.fori_loop(0, counts[widest], step, 0)


def chunk_of(sel, place, lead=()):
    return (*lead, *(first + at for (first, _), at in zip(sel, place)), pl.ds(*sel[3]), slice(None))


def as_f32(value):
    return value.astype(jnp.float32)


def reduce_kernel(*refs):
    terms_ref, out_ref, held, other, final = refs[:5]
    landing = {}
    at = 5
    for part in range(len(PARTS)):
        for stage in range(3):
            landing[part, stage] = refs[at]
            at += 1
    send, recv, load_sem, side_send, side_recv, last_send, last_recv = refs[at:]
    pos, me, core = my_place()
    sibling = (me, 1 - core)
    greet(pos, me, core)

    def load(z):
        return pltpu.make_async_copy(terms_ref.at[core, z], held.at[z], load_sem.at[z])

    def side(z):
        return pltpu.make_async_remote_copy(
            src_ref=terms_ref.at[1 - core, z],
            dst_ref=other.at[z],
            send_sem=side_send.at[z],
            recv_sem=side_recv.at[z],
            device_id=sibling,
            device_id_type=MESH,
        )

    for z in range(SIZES["z"]):
        side(z).start()
        load(z).start()
    for z in range(SIZES["z"]):
        load(z).wait()
        side(z).wait_recv()

        def join(place, z=z):
            where = (z, place[1], place[2])
            held[where] = (as_f32(held[where]) + as_f32(other[where])).astype(jnp.bfloat16)

        each_chunk((1, SIZES["y"], SIZES["x"]), join)

    def copy(part, stage, step, way, arriving):
        axis = PARTS[part][2][::-1][stage]
        toward = 1 - 2 * way
        size = SIZES[axis]
        reach = size // 2 - step + (0 if arriving else 1)
        index = wrapped(pos[axis] + toward * reach, size)
        half = way if step == 1 else None
        from_sel, to_sel = sum_views(pos, part, stage, index, half)
        return pltpu.make_async_remote_copy(
            src_ref=held.at[spans(from_sel)],
            dst_ref=landing[part, stage].at[(way, *spans(to_sel))],
            send_sem=send.at[part, stage, step - 1, way],
            recv_sem=recv.at[part, stage, step - 1, way],
            device_id=ring_peer(pos, core, axis, toward),
            device_id_type=MESH,
        )

    def add_arrived(part, stage, step, way):
        axis = PARTS[part][2][::-1][stage]
        toward = 1 - 2 * way
        size = SIZES[axis]
        index = wrapped(pos[axis] + toward * (size // 2 - step), size)
        half = way if step == 1 else None
        into, arrived = sum_views(pos, part, stage, index, half)
        landed = landing[part, stage]

        def add(place):
            where = chunk_of(into, place)
            more = landed[chunk_of(arrived, place, (way,))]
            held[where] = (as_f32(held[where]) + as_f32(more)).astype(jnp.bfloat16)

        each_chunk([count for _, count in into[:3]], add)

    def add_both(part, stage, step):
        axis = PARTS[part][2][::-1][stage]
        into, arrived = sum_views(pos, part, stage, pos[axis], None)
        landed = landing[part, stage]

        def add(place):
            where = chunk_of(into, place)
            total = as_f32(held[where])
            total = total + as_f32(landed[chunk_of(arrived, place, (0,))])
            total = total + as_f32(landed[chunk_of(arrived, place, (1,))])
            held[where] = total.astype(jnp.bfloat16)

        each_chunk([count for _, count in into[:3]], add)

    plans = [ring_steps(order[::-1]) for _, _, order in PARTS]
    longest = max(len(plan) for plan in plans)
    for slot in range(longest + 1):
        for part, plan in enumerate(plans):
            if slot > len(plan):
                continue
            if slot > 0:
                stage, step = plan[slot - 1]
                for way in (0, 1):
                    copy(part, stage, step, way, True).wait_recv()
                last_step = step == SIZES[PARTS[part][2][::-1][stage]] // 2
                if last_step and step > 1:
                    add_both(part, stage, step)
                else:
                    for way in (0, 1):
                        add_arrived(part, stage, step, way)
            if slot < len(plan):
                for way in (0, 1):
                    copy(part, *plan[slot], way, False).start()

    final[core] = held[pos["z"], pos["y"], pos["x"]]
    last = pltpu.make_async_remote_copy(
        src_ref=final.at[core],
        dst_ref=final.at[core],
        send_sem=last_send,
        recv_sem=last_recv,
        device_id=sibling,
        device_id_type=MESH,
    )
    last.start()
    for z in range(SIZES["z"]):
        side(z).wait_send()
    for part, plan in enumerate(plans):
        for stage, step in plan:
            for way in (0, 1):
                copy(part, stage, step, way, False).wait_send()
    last.wait()
    out_ref[...] = final[...]


def reduce_all(terms):
    dims = tuple(SIZES[axis] for axis in AXES)
    whole = pltpu.VMEM((*dims, 2 * SPAN, HD), jnp.bfloat16)
    sems = pltpu.SemaphoreType.DMA((len(PARTS), 3, 4, 2))
    by_z = pltpu.SemaphoreType.DMA((SIZES["z"],))
    return pl.pallas_call(
        reduce_kernel,
        out_shape=jax.ShapeDtypeStruct((2, 2 * SPAN, HD), jnp.bfloat16),
        in_specs=[pl.BlockSpec(memory_space=pl.ANY)],
        out_specs=pl.BlockSpec(memory_space=pltpu.VMEM),
        scratch_shapes=[whole, whole, pltpu.VMEM((2, 2 * SPAN, HD), jnp.bfloat16)]
        + [
            pltpu.VMEM(landing_shape(part, stage), jnp.bfloat16)
            for part in range(len(PARTS))
            for stage in range(3)
        ]
        + [sems, sems, by_z, by_z, by_z, pltpu.SemaphoreType.DMA, pltpu.SemaphoreType.DMA],
        compiler_params=pltpu.CompilerParams(
            collective_id=1, has_side_effects=True, vmem_limit_bytes=VMEM_BYTES
        ),
    )(terms)


def dot(left, right, contract):
    return lax.dot_general(
        left, right, ((contract[:1], contract[1:]), ((), ())), preferred_element_type=jnp.float32
    )


def attention_kernel(
    place_ref, starts_ref, spans_ref, q_ref, g_ref, kv_ref, out_ref, dq_ref, terms_ref,
    scores, probs, q_cols, g_cols, acc,
):
    heads = q_ref.shape[1] // HD
    cols = heads * SPAN
    scale = 1.0 / math.sqrt(HD)
    to_exp2 = scale * math.log2(math.e)
    per_block = BLOCK // SPAN

    def clear(at, carry):
        terms_ref[:, pl.ds(pl.multiple_of(at * 256, 256), 256), :] = jnp.zeros((2, 256, HD), jnp.bfloat16)
        return carry

    lax.fori_loop(0, terms_ref.shape[1] // 256, clear, 0)

    for part in range(2):
        base = spans_ref[part] * SPAN
        doc_first = jnp.int32(0)
        for doc in range(starts_ref.shape[0]):
            start = starts_ref[doc]
            doc_first = jnp.where(start <= base, jnp.maximum(doc_first, start), doc_first)
        first_block = doc_first // BLOCK
        full_blocks = base // BLOCK - first_block
        inside = base - (base // BLOCK) * BLOCK

        rows = pl.ds(part * SPAN, SPAN)
        q_rows = jnp.concatenate(
            [q_ref[rows, h * HD : (h + 1) * HD] for h in range(heads)], axis=0
        )
        g_rows = jnp.concatenate(
            [g_ref[rows, h * HD : (h + 1) * HD] for h in range(heads)], axis=0
        )
        q_t = as_f32(q_rows).T
        g_t = as_f32(g_rows).T
        q_cols[...] = q_t.astype(jnp.bfloat16)
        g_cols[...] = g_t.astype(jnp.bfloat16)

        def row_of(block, i):
            span = place_ref[(first_block + block) * per_block + i]
            return pl.ds(pl.multiple_of(span * SPAN, SPAN), SPAN)

        def tile(which, block):
            return jnp.concatenate(
                [kv_ref[which, row_of(block, i), :] for i in range(per_block)], axis=0
            )

        def fold(value, op):
            value = value.reshape(BLOCK // 8, 8, cols)
            return op(value, axis=0)

        def score_step(block, top):
            s = dot(tile(0, block), q_cols[...], (1, 0))
            scores[block] = s
            return jnp.maximum(top, fold(s, jnp.max))

        top = lax.fori_loop(0, full_blocks, score_step, jnp.full((8, cols), -1e30, jnp.float32))
        s = dot(tile(0, full_blocks), q_cols[...], (1, 0))
        key_at = lax.broadcasted_iota(jnp.int32, (BLOCK, cols), 0)
        query_at = lax.broadcasted_iota(jnp.int32, (BLOCK, cols), 1)
        s = jnp.where(key_at <= inside + lax.rem(query_at, SPAN), s, -1e30)
        scores[full_blocks] = s
        top = jnp.max(jnp.maximum(top, fold(s, jnp.max)), axis=0, keepdims=True)

        acc[...] = jnp.zeros_like(acc)

        def value_step(block, total):
            p = jnp.exp2((scores[block] - top) * to_exp2)
            p16 = p.astype(jnp.bfloat16)
            probs[block] = p16
            acc[...] += dot(tile(1, block), p16, (0, 0))
            return total + fold(p, jnp.sum)

        total = lax.fori_loop(0, full_blocks + 1, value_step, jnp.zeros((8, cols), jnp.float32))
        inverse = 1.0 / jnp.sum(total, axis=0, keepdims=True)
        out_t = (acc[...] * inverse).astype(jnp.bfloat16).astype(jnp.float32)
        delta = jnp.sum(g_t * out_t, axis=0, keepdims=True)
        q_scaled = (q_t * (inverse * scale)).astype(jnp.bfloat16)
        g_scaled = (g_t * inverse).astype(jnp.bfloat16)
        out_rows = out_t.T.astype(jnp.bfloat16)
        acc[...] = jnp.zeros_like(acc)

        def grad_step(block, carry):
            p16 = probs[block]
            keys = tile(0, block)
            d_probs = dot(tile(1, block), g_cols[...], (1, 0))
            d_scores = (as_f32(p16) * (d_probs - delta)).astype(jnp.bfloat16)
            acc[...] += dot(keys, d_scores, (0, 0))
            d_key = dot(d_scores, q_scaled, (1, 1))
            d_value = dot(p16, g_scaled, (1, 1))
            for i in range(per_block):
                at = row_of(block, i)
                for which, term in ((0, d_key), (1, d_value)):
                    piece = term[i * SPAN : (i + 1) * SPAN]
                    if part > 0:
                        piece = piece + as_f32(terms_ref[which, at, :])
                    terms_ref[which, at, :] = piece.astype(jnp.bfloat16)
            return carry

        lax.fori_loop(0, full_blocks + 1, grad_step, 0)
        dq_rows = (acc[...] * (inverse * scale)).T.astype(jnp.bfloat16)
        for h in range(heads):
            out_ref[rows, h * HD : (h + 1) * HD] = out_rows[h * SPAN : (h + 1) * SPAN]
            dq_ref[rows, h * HD : (h + 1) * HD] = dq_rows[h * SPAN : (h + 1) * SPAN]


def attention(place, doc_starts, my_spans, queries, d_out, kv_all):
    tokens = kv_all.shape[1]
    heads = queries.shape[1] // HD
    cols = heads * SPAN
    longest = tokens - (doc_starts.shape[0] - 1) * UNIT
    blocks = -(-longest // BLOCK)
    smem = pl.BlockSpec(memory_space=pltpu.SMEM)
    vmem = pl.BlockSpec(memory_space=pltpu.VMEM)
    return pl.pallas_call(
        attention_kernel,
        out_shape=(
            jax.ShapeDtypeStruct(queries.shape, jnp.bfloat16),
            jax.ShapeDtypeStruct(queries.shape, jnp.bfloat16),
            jax.ShapeDtypeStruct((2, tokens, HD), jnp.bfloat16),
        ),
        in_specs=[smem, smem, smem, vmem, vmem, vmem],
        out_specs=(vmem, vmem, vmem),
        scratch_shapes=[
            pltpu.VMEM((blocks, BLOCK, cols), jnp.float32),
            pltpu.VMEM((blocks, BLOCK, cols), jnp.bfloat16),
            pltpu.VMEM((HD, cols), jnp.bfloat16),
            pltpu.VMEM((HD, cols), jnp.bfloat16),
            pltpu.VMEM((HD, cols), jnp.float32),
        ],
        compiler_params=pltpu.CompilerParams(vmem_limit_bytes=VMEM_BYTES),
    )(place, doc_starts, my_spans, queries, d_out, kv_all)


def body(queries, keys, values, d_out, doc_starts, assign):
    span_total = assign.shape[0]
    tokens = span_total * SPAN
    rows_dev = queries.shape[0]
    dims = tuple(SIZES[axis] for axis in AXES)
    kv = jnp.stack([keys, values]).reshape(2, 1, 1, 1, rows_dev, HD)
    ids = jnp.arange(span_total, dtype=jnp.int32)
    place = jnp.sum(jnp.where(assign[None, :] == ids[:, None], ids[None, :], 0), axis=1)
    my_spans = lax.dynamic_slice_in_dim(assign, lax.axis_index("ctx") * 2, 2, 0)
    kv_all = gather_all(kv).reshape(2, tokens, HD)
    attn_out, d_query, terms = attention(place, doc_starts, my_spans, queries, d_out, kv_all)
    summed = reduce_all(terms.reshape(2, *dims, rows_dev, HD))
    return (attn_out, d_query, summed[0], summed[1])


def solution(mesh):
    placed = (P("ctx", "head"), P("ctx", None), P("ctx", None), P("ctx", "head"), P(), P())
    return jax.shard_map(
        body,
        mesh=mesh,
        in_specs=placed,
        out_specs=(P("ctx", "head"), P("ctx", "head"), P("ctx", None), P("ctx", None)),
        check_vma=False,
    )
```

```python
import math

import jax
import jax.numpy as jnp
from jax import lax
from jax.experimental import pallas as pl
from jax.experimental.pallas import tpu as pltpu
from jax.sharding import PartitionSpec as P

HD = 128
SPAN = 64
ROWS = 2 * SPAN
BLOCK = 512
UNIT = 512
MESH = pl.DeviceIdType.MESH
AXES = ("z", "y", "x")
SIZES = {"z": 8, "y": 4, "x": 4}
ROUTE_A = (0, 32)
ROUTES = ((32, 48, "y", "x"), (80, 48, "x", "y"))
NEAR = (1, -1, 2)
Z_AWAY = (1, -1, 2, -2, 3, -3, 4)
GROUPS = ((0,), (1, -1), (2, -2), (3, -3), (4,))
COPIES = 160
VMEM_BYTES = 60 * 1024 * 1024


def my_place():
    me = lax.axis_index("ctx")
    nx, ny = SIZES["x"], SIZES["y"]
    pos = {"x": lax.rem(me, nx), "y": lax.rem(me // nx, ny), "z": me // (nx * ny)}
    return pos, me, lax.axis_index("head")


def wrapped(value, size):
    return lax.rem(value + 2 * size, size)


def shifted(pos, axis, step):
    return wrapped(pos[axis] + step, SIZES[axis])


def peer(pos, core, axis, step):
    there = dict(pos)
    there[axis] = shifted(pos, axis, step)
    return ((there["z"] * SIZES["y"] + there["y"]) * SIZES["x"] + there["x"], core)


def greet(pos, me, core):
    barrier = pltpu.get_barrier_semaphore()
    partners = [("z", step) for step in Z_AWAY] + [(axis, step) for axis in "yx" for step in NEAR]
    for axis, step in partners:
        pl.semaphore_signal(
            barrier, inc=1, device_id=peer(pos, core, axis, step), device_id_type=MESH
        )
    pl.semaphore_signal(barrier, inc=1, device_id=(me, 1 - core), device_id_type=MESH)
    pl.semaphore_wait(barrier, len(partners) + 1)


def as_f32(value):
    return value.astype(jnp.float32)


class Numbers(dict):
    def __missing__(self, key):
        self[key] = len(self)
        assert len(self) <= COPIES
        return self[key]


def gather_kernel(k_ref, v_ref, all_ref, send, recv, side_send, side_recv, local_sem):
    pos, me, core = my_place()
    here = tuple(pl.ds(pos[axis], 1) for axis in AXES)
    own_copies = [
        pltpu.make_async_copy(ref, all_ref.at[(which, *here)], local_sem.at[which])
        for which, ref in ((0, k_ref), (1, v_ref))
    ]
    for copy in own_copies:
        copy.start()
    greet(pos, me, core)
    for copy in own_copies:
        copy.wait()

    number = Numbers()
    started, passed = [], []

    def view(owner, rows, **sel):
        index = [sel[axis] if axis in sel else (pos[axis], 1) for axis in AXES]
        return all_ref.at[(owner, *(pl.ds(*at) for at in index), pl.ds(*rows), slice(None))]

    def copy(key, axis, step, rows, sel):
        ref = view(core, rows, **sel)
        at = number[key]
        return pltpu.make_async_remote_copy(
            src_ref=ref, dst_ref=ref, send_sem=send.at[at], recv_sem=recv.at[at],
            device_id=peer(pos, core, axis, step), device_id_type=MESH,
        )

    def side(key, owner, rows, sel):
        ref = view(owner, rows, **sel)
        at = number[key]
        return pltpu.make_async_remote_copy(
            src_ref=ref, dst_ref=ref, send_sem=side_send.at[at], recv_sem=side_recv.at[at],
            device_id=(me, 1 - core), device_id_type=MESH,
        )

    def push(key, axis, step, rows, sel):
        copy(key, axis, step, rows, sel).start()
        started.append((key, axis, step, rows, sel))

    def arrive(key, axis, step, rows, sel):
        copy(key, axis, step, rows, sel).wait_recv()
        side(key, core, rows, sel).start()
        passed.append((key, rows, sel))

    def full(axis):
        return (0, SIZES[axis])

    def half(axis, side_at):
        return (side_at * (SIZES[axis] // 2), SIZES[axis] // 2)

    def from_z(route, d):
        first, count, _, _ = ROUTES[route]
        step = 4 if d == 4 else -d
        arrive(("z", route, d), "z", step, (first, count), {"z": (shifted(pos, "z", d), 1)})

    def to_z(route, d):
        first, count, _, _ = ROUTES[route]
        step = 4 if d == 4 else -d
        push(("z", route, d), "z", step, (first, count), {})

    def to_middle(route, d):
        first, count, middle, _ = ROUTES[route]
        for m in NEAR:
            push(("m", route, d, m), middle, m, (first, count), {"z": (shifted(pos, "z", d), 1)})

    def from_middle(route, d):
        first, count, middle, _ = ROUTES[route]
        for m in NEAR:
            sel = {"z": (shifted(pos, "z", d), 1), middle: (shifted(pos, middle, -m), 1)}
            arrive(("m", route, d, m), middle, m, (first, count), sel)

    def to_last(route, d):
        first, count, middle, last = ROUTES[route]
        for way in (0, 1):
            sel = {"z": (shifted(pos, "z", d), 1), middle: full(middle)}
            push(("l", route, d, way), last, 1 - 2 * way, (first, count), sel)

    def pass_last(route, d):
        first, count, middle, last = ROUTES[route]
        for way in (0, 1):
            toward = 1 - 2 * way
            sel = {"z": (shifted(pos, "z", d), 1), middle: full(middle),
                   last: (shifted(pos, last, -toward), 1)}
            arrive(("l", route, d, way), last, toward, (first, count), sel)
            sel = dict(sel, **{middle: half(middle, way)})
            push(("p", route, d, way), last, toward, (first, count), sel)

    def from_last(route, d):
        first, count, middle, last = ROUTES[route]
        for way in (0, 1):
            toward = 1 - 2 * way
            sel = {"z": (shifted(pos, "z", d), 1), middle: half(middle, way),
                   last: (shifted(pos, last, -2 * toward), 1)}
            arrive(("p", route, d, way), last, toward, (first, count), sel)

    def ring_sel(part, step, way, arriving):
        toward = 1 - 2 * way
        back = step if arriving else step - 1
        sel = {"z": (shifted(pos, "z", -toward * back), 1), "y": half("y", part), "x": full("x")}
        if step == SIZES["z"] // 2:
            sel["x"] = half("x", way)
        return sel

    def a_ring(step):
        for part in (0, 1):
            for way in (0, 1):
                toward = 1 - 2 * way
                if step > 1:
                    arrive(("r", part, step - 1, way), "z", toward, ROUTE_A, ring_sel(part, step - 1, way, True))
                if step <= SIZES["z"] // 2:
                    push(("r", part, step, way), "z", toward, ROUTE_A, ring_sel(part, step, way, False))

    both = range(len(ROUTES))
    for m in NEAR:
        push(("y", m), "y", m, ROUTE_A, {})
    for group in GROUPS[1:]:
        for route in both:
            for d in group:
                to_z(route, d)
    for route in both:
        to_middle(route, 0)
    for m in NEAR:
        arrive(("y", m), "y", m, ROUTE_A, {"y": (shifted(pos, "y", -m), 1)})
    for m in NEAR:
        push(("x", m), "x", m, ROUTE_A, {"y": full("y")})
    for at in range(len(GROUPS) + 2):
        if at + 1 < len(GROUPS):
            for route in both:
                for d in GROUPS[at + 1]:
                    from_z(route, d)
                    to_middle(route, d)
        if at < len(GROUPS):
            for route in both:
                for d in GROUPS[at]:
                    from_middle(route, d)
                    to_last(route, d)
        if at == 0:
            for m in NEAR:
                arrive(("x", m), "x", m, ROUTE_A, {"y": full("y"), "x": (shifted(pos, "x", -m), 1)})
        if at <= SIZES["z"] // 2:
            a_ring(at + 1)
        if 0 < at <= len(GROUPS):
            for route in both:
                for d in GROUPS[at - 1]:
                    pass_last(route, d)
        if 1 < at:
            for route in both:
                for d in GROUPS[at - 2]:
                    from_last(route, d)
    for item in started:
        copy(*item).wait_send()
    for key, rows, sel in passed:
        side(key, core, rows, sel).wait_send()
        side(key, 1 - core, rows, sel).wait_recv()


def gather_all(keys, values):
    dims = tuple(SIZES[axis] for axis in AXES)
    sems = pltpu.SemaphoreType.DMA((COPIES,))
    anywhere = pl.BlockSpec(memory_space=pl.ANY)
    return pl.pallas_call(
        gather_kernel,
        out_shape=jax.ShapeDtypeStruct((2, *dims, ROWS, HD), jnp.bfloat16),
        in_specs=[anywhere, anywhere],
        out_specs=anywhere,
        scratch_shapes=[sems, sems, sems, sems, pltpu.SemaphoreType.DMA((2,))],
        compiler_params=pltpu.CompilerParams(collective_id=0, has_side_effects=True),
    )(keys.reshape(1, 1, 1, ROWS, HD), values.reshape(1, 1, 1, ROWS, HD))


def reduce_kernel(
    terms_ref, out_ref, held, other, final, ring_land, ax_land, ay_land, first_land, second_land,
    middle_land, z_land, send, recv, load_sem, side_send, side_recv, last_send, last_recv,
):
    pos, me, core = my_place()
    sibling = (me, 1 - core)

    def load(d):
        z = shifted(pos, "z", d)
        return pltpu.make_async_copy(terms_ref.at[core, z], held.at[z], load_sem.at[d % 8])

    def side(d):
        z = shifted(pos, "z", d)
        return pltpu.make_async_remote_copy(
            src_ref=terms_ref.at[1 - core, z], dst_ref=other.at[z],
            send_sem=side_send.at[d % 8], recv_sem=side_recv.at[d % 8],
            device_id=sibling, device_id_type=MESH,
        )

    far_first = GROUPS[::-1]
    for group in far_first:
        for d in group:
            load(d).start()
    greet(pos, me, core)
    for group in far_first:
        for d in group:
            side(d).start()

    number = Numbers()
    started = []

    def copy(key, axis, step, src, dst):
        at = number[key]
        return pltpu.make_async_remote_copy(
            src_ref=src, dst_ref=dst, send_sem=send.at[at], recv_sem=recv.at[at],
            device_id=peer(pos, core, axis, step), device_id_type=MESH,
        )

    def push(*item):
        copy(*item).start()
        started.append(item)

    def held_at(rows, **sel):
        index = []
        for axis in AXES:
            at = sel[axis] if axis in sel else pos[axis]
            index.append(pl.ds(*at) if isinstance(at, tuple) else at)
        return (*index, pl.ds(*rows), slice(None))

    def add(where, lands):
        total = as_f32(held[where])
        for land in lands:
            total = total + as_f32(land[...])
        held[where] = total.astype(jnp.bfloat16)

    def join(d):
        load(d).wait()
        side(d).wait_recv()
        z = shifted(pos, "z", d)

        def one(y, carry):
            for x in range(SIZES["x"]):
                held[z, y, x] = (as_f32(held[z, y, x]) + as_f32(other[z, y, x])).astype(jnp.bfloat16)
            return carry

        lax.fori_loop(0, SIZES["y"], one, 0)

    def middle_half(middle, way):
        size = SIZES[middle] // 2
        return (way * size, size)

    def first_copy(route, d, way):
        first, count, middle, last = ROUTES[route]
        where = {"z": shifted(pos, "z", d), middle: middle_half(middle, way), last: shifted(pos, last, 2)}
        return (("f", route, d, way), last, 1 - 2 * way, held.at[held_at((first, count), **where)],
                first_land.at[route, d % 8, way])

    def second_copy(route, d, way):
        first, count, middle, last = ROUTES[route]
        where = {"z": shifted(pos, "z", d), middle: (0, SIZES[middle]), last: shifted(pos, last, 1 - 2 * way)}
        return (("s", route, d, way), last, 1 - 2 * way, held.at[held_at((first, count), **where)],
                second_land.at[route, d % 8, way])

    def middle_copy(route, d, m):
        first, count, middle, last = ROUTES[route]
        where = {"z": shifted(pos, "z", d), middle: shifted(pos, middle, m)}
        return (("m", route, d, m), middle, m, held.at[held_at((first, count), **where)],
                middle_land.at[route, d % 8, NEAR.index(m)])

    def z_copy(route, d):
        first, count, _, _ = ROUTES[route]
        return (("z", route, d), "z", d, held.at[held_at((first, count), z=shifted(pos, "z", d))],
                z_land.at[route, Z_AWAY.index(d)])

    def send_first(route, d):
        for way in (0, 1):
            push(*first_copy(route, d, way))

    def send_second(route, d):
        first, count, middle, last = ROUTES[route]
        for way in (0, 1):
            copy(*first_copy(route, d, way)).wait_recv()
            low, size = middle_half(middle, way)
            for i in range(size):
                where = {"z": shifted(pos, "z", d), middle: low + i, last: shifted(pos, last, 1 - 2 * way)}
                add(held_at((first, count), **where), [first_land.at[route, d % 8, way, i]])
            push(*second_copy(route, d, way))

    def send_middle(route, d):
        first, count, middle, last = ROUTES[route]
        for way in (0, 1):
            copy(*second_copy(route, d, way)).wait_recv()
        for i in range(SIZES[middle]):
            where = {"z": shifted(pos, "z", d), middle: i}
            add(held_at((first, count), **where), [second_land.at[route, d % 8, way, i] for way in (0, 1)])
        for m in NEAR:
            push(*middle_copy(route, d, m))

    def send_z(route, d):
        first, count, _, _ = ROUTES[route]
        for m in NEAR:
            copy(*middle_copy(route, d, m)).wait_recv()
        where = held_at((first, count), z=shifted(pos, "z", d))
        add(where, [middle_land.at[route, d % 8, i] for i in range(len(NEAR))])
        if d != 0:
            push(*z_copy(route, d))

    def ring_copy(step, way):
        toward = 1 - 2 * way
        half = SIZES["x"] // 2
        xs = (way * half, half) if step == 1 else (0, SIZES["x"])
        where = {"z": shifted(pos, "z", toward * (5 - step)), "y": (0, SIZES["y"]), "x": xs}
        return (("r", step, way), "z", toward, held.at[held_at(ROUTE_A, **where)],
                ring_land.at[way, step - 1, :, pl.ds(*xs)])

    def ring(step):
        for way in (0, 1):
            toward = 1 - 2 * way
            half = SIZES["x"] // 2
            if 1 < step < 5:
                copy(*ring_copy(step - 1, way)).wait_recv()
                low, size = (way * half, half) if step == 2 else (0, SIZES["x"])
                z = shifted(pos, "z", toward * (5 - step))

                def one(y, carry):
                    for i in range(size):
                        add(held_at(ROUTE_A, z=z, y=y, x=low + i), [ring_land.at[way, step - 2, y, low + i]])
                    return carry

                lax.fori_loop(0, SIZES["y"], one, 0)
            if step < 5:
                push(*ring_copy(step, way))
        if step == 5:
            for way in (0, 1):
                copy(*ring_copy(4, way)).wait_recv()

            def last(y, carry):
                for x in range(SIZES["x"]):
                    add(held_at(ROUTE_A, y=y, x=x), [ring_land.at[way, 3, y, x] for way in (0, 1)])
                return carry

            lax.fori_loop(0, SIZES["y"], last, 0)

    def ax_copy(m):
        where = {"y": (0, SIZES["y"]), "x": shifted(pos, "x", m)}
        return (("ax", m), "x", m, held.at[held_at(ROUTE_A, **where)], ax_land.at[NEAR.index(m)])

    def ay_copy(m):
        where = {"y": shifted(pos, "y", m)}
        return (("ay", m), "y", m, held.at[held_at(ROUTE_A, **where)], ay_land.at[NEAR.index(m)])

    both = range(len(ROUTES))
    for at in range(len(far_first) + 3):
        if at < len(far_first):
            for d in far_first[at]:
                join(d)
            for route in both:
                for d in far_first[at]:
                    send_first(route, d)
            ring(at + 1)
        if at == len(far_first) - 1:
            for m in NEAR:
                push(*ax_copy(m))
        for behind, act in ((1, send_second), (2, send_middle), (3, send_z)):
            if 0 <= at - behind < len(far_first):
                for route in both:
                    for d in far_first[at - behind]:
                        act(route, d)
        if at == len(far_first):
            for m in NEAR:
                copy(*ax_copy(m)).wait_recv()
            for y in range(SIZES["y"]):
                add(held_at(ROUTE_A, y=y), [ax_land.at[i, y] for i in range(len(NEAR))])
            for m in NEAR:
                push(*ay_copy(m))
    for m in NEAR:
        copy(*ay_copy(m)).wait_recv()
    add(held_at(ROUTE_A), [ay_land.at[i] for i in range(len(NEAR))])
    for route in both:
        first, count, _, _ = ROUTES[route]
        for d in Z_AWAY:
            copy(*z_copy(route, d)).wait_recv()
        add(held_at((first, count)), [z_land.at[route, i] for i in range(len(Z_AWAY))])

    final[core] = held[pos["z"], pos["y"], pos["x"]]
    last_copy = pltpu.make_async_remote_copy(
        src_ref=final.at[core], dst_ref=final.at[core], send_sem=last_send, recv_sem=last_recv,
        device_id=sibling, device_id_type=MESH,
    )
    last_copy.start()
    for group in far_first:
        for d in group:
            side(d).wait_send()
    for item in started:
        copy(*item).wait_send()
    last_copy.wait()
    out_ref[...] = final[...]


def reduce_all(terms):
    dims = tuple(SIZES[axis] for axis in AXES)
    nz, ny, nx = dims

    def vmem(*shape):
        return pltpu.VMEM((*shape, HD), jnp.bfloat16)

    count = ROUTES[0][1]
    routes = len(ROUTES)
    sems = pltpu.SemaphoreType.DMA((COPIES,))
    by_z = pltpu.SemaphoreType.DMA((nz,))
    return pl.pallas_call(
        reduce_kernel,
        out_shape=jax.ShapeDtypeStruct((2, ROWS, HD), jnp.bfloat16),
        in_specs=[pl.BlockSpec(memory_space=pl.ANY)],
        out_specs=pl.BlockSpec(memory_space=pltpu.VMEM),
        scratch_shapes=[
            vmem(*dims, ROWS),
            vmem(*dims, ROWS),
            vmem(2, ROWS),
            vmem(2, nz // 2, ny, nx, ROUTE_A[1]),
            vmem(len(NEAR), ny, ROUTE_A[1]),
            vmem(len(NEAR), ROUTE_A[1]),
            vmem(routes, nz, 2, 2, count),
            vmem(routes, nz, 2, 4, count),
            vmem(routes, nz, len(NEAR), count),
            vmem(routes, len(Z_AWAY), count),
            sems, sems, by_z, by_z, by_z, pltpu.SemaphoreType.DMA, pltpu.SemaphoreType.DMA,
        ],
        compiler_params=pltpu.CompilerParams(
            collective_id=1, has_side_effects=True, vmem_limit_bytes=VMEM_BYTES
        ),
    )(terms)


def dot(left, right, contract):
    return lax.dot_general(
        left, right, ((contract[:1], contract[1:]), ((), ())), preferred_element_type=jnp.float32
    )


def attention_kernel(
    starts_ref, assign_ref, q_ref, g_ref, kv_ref, out_ref, dq_ref, terms_ref,
    place_ref, scores, probs, q_cols, g_cols, acc,
):
    heads = q_ref.shape[1] // HD
    cols = heads * SPAN
    scale = 1.0 / math.sqrt(HD)
    to_exp2 = scale * math.log2(math.e)
    per_block = BLOCK // SPAN

    def clear(at, carry):
        terms_ref[:, pl.ds(pl.multiple_of(at * 256, 256), 256), :] = jnp.zeros((2, 256, HD), jnp.bfloat16)
        return carry

    lax.fori_loop(0, terms_ref.shape[1] // 256, clear, 0)

    def locate(at, carry):
        for i in range(8):
            place_ref[assign_ref[at * 8 + i]] = at * 8 + i
        return carry

    lax.fori_loop(0, assign_ref.shape[0] // 8, locate, 0)
    first_span = lax.axis_index("ctx") * 2

    for part in range(2):
        base = assign_ref[first_span + part] * SPAN
        doc_first = jnp.int32(0)
        for doc in range(starts_ref.shape[0]):
            start = starts_ref[doc]
            doc_first = jnp.where(start <= base, jnp.maximum(doc_first, start), doc_first)
        first_block = doc_first // BLOCK
        full_blocks = base // BLOCK - first_block
        inside = base - (base // BLOCK) * BLOCK

        rows = pl.ds(part * SPAN, SPAN)
        q_rows = jnp.concatenate(
            [q_ref[rows, h * HD : (h + 1) * HD] for h in range(heads)], axis=0
        )
        g_rows = jnp.concatenate(
            [g_ref[rows, h * HD : (h + 1) * HD] for h in range(heads)], axis=0
        )
        q_t = as_f32(q_rows).T
        g_t = as_f32(g_rows).T
        q_cols[...] = q_t.astype(jnp.bfloat16)
        g_cols[...] = g_t.astype(jnp.bfloat16)

        def row_of(block, i):
            span = place_ref[(first_block + block) * per_block + i]
            return pl.ds(pl.multiple_of(span * SPAN, SPAN), SPAN)

        def tile(which, block):
            return jnp.concatenate(
                [kv_ref[which, row_of(block, i), :] for i in range(per_block)], axis=0
            )

        def fold(value, op):
            value = value.reshape(BLOCK // 8, 8, cols)
            return op(value, axis=0)

        def score_step(block, top):
            s = dot(tile(0, block), q_cols[...], (1, 0))
            scores[block] = s
            return jnp.maximum(top, fold(s, jnp.max))

        top = lax.fori_loop(0, full_blocks, score_step, jnp.full((8, cols), -1e30, jnp.float32))
        s = dot(tile(0, full_blocks), q_cols[...], (1, 0))
        key_at = lax.broadcasted_iota(jnp.int32, (BLOCK, cols), 0)
        query_at = lax.broadcasted_iota(jnp.int32, (BLOCK, cols), 1)
        s = jnp.where(key_at <= inside + lax.rem(query_at, SPAN), s, -1e30)
        scores[full_blocks] = s
        top = jnp.max(jnp.maximum(top, fold(s, jnp.max)), axis=0, keepdims=True)

        acc[...] = jnp.zeros_like(acc)

        def value_step(block, total):
            p = jnp.exp2((scores[block] - top) * to_exp2)
            p16 = p.astype(jnp.bfloat16)
            probs[block] = p16
            acc[...] += dot(tile(1, block), p16, (0, 0))
            return total + fold(p, jnp.sum)

        total = lax.fori_loop(0, full_blocks + 1, value_step, jnp.zeros((8, cols), jnp.float32))
        inverse = 1.0 / jnp.sum(total, axis=0, keepdims=True)
        out_t = (acc[...] * inverse).astype(jnp.bfloat16).astype(jnp.float32)
        delta = jnp.sum(g_t * out_t, axis=0, keepdims=True)
        q_scaled = (q_t * (inverse * scale)).astype(jnp.bfloat16)
        g_scaled = (g_t * inverse).astype(jnp.bfloat16)
        out_rows = out_t.T.astype(jnp.bfloat16)
        acc[...] = jnp.zeros_like(acc)

        def grad_step(block, carry):
            p16 = probs[block]
            keys = tile(0, block)
            d_probs = dot(tile(1, block), g_cols[...], (1, 0))
            d_scores = (as_f32(p16) * (d_probs - delta)).astype(jnp.bfloat16)
            acc[...] += dot(keys, d_scores, (0, 0))
            d_key = dot(d_scores, q_scaled, (1, 1))
            d_value = dot(p16, g_scaled, (1, 1))
            for i in range(per_block):
                at = row_of(block, i)
                for which, term in ((0, d_key), (1, d_value)):
                    piece = term[i * SPAN : (i + 1) * SPAN]
                    if part > 0:
                        piece = piece + as_f32(terms_ref[which, at, :])
                    terms_ref[which, at, :] = piece.astype(jnp.bfloat16)
            return carry

        lax.fori_loop(0, full_blocks + 1, grad_step, 0)
        dq_rows = (acc[...] * (inverse * scale)).T.astype(jnp.bfloat16)
        for h in range(heads):
            out_ref[rows, h * HD : (h + 1) * HD] = out_rows[h * SPAN : (h + 1) * SPAN]
            dq_ref[rows, h * HD : (h + 1) * HD] = dq_rows[h * SPAN : (h + 1) * SPAN]


def attention(doc_starts, assign, queries, d_out, kv_all):
    tokens = kv_all.shape[1]
    heads = queries.shape[1] // HD
    cols = heads * SPAN
    longest = tokens - (doc_starts.shape[0] - 1) * UNIT
    blocks = -(-longest // BLOCK)
    smem = pl.BlockSpec(memory_space=pltpu.SMEM)
    vmem = pl.BlockSpec(memory_space=pltpu.VMEM)
    return pl.pallas_call(
        attention_kernel,
        out_shape=(
            jax.ShapeDtypeStruct(queries.shape, jnp.bfloat16),
            jax.ShapeDtypeStruct(queries.shape, jnp.bfloat16),
            jax.ShapeDtypeStruct((2, tokens, HD), jnp.bfloat16),
        ),
        in_specs=[smem, smem, vmem, vmem, vmem],
        out_specs=(vmem, vmem, vmem),
        scratch_shapes=[
            pltpu.SMEM(assign.shape, jnp.int32),
            pltpu.VMEM((blocks, BLOCK, cols), jnp.float32),
            pltpu.VMEM((blocks, BLOCK, cols), jnp.bfloat16),
            pltpu.VMEM((HD, cols), jnp.bfloat16),
            pltpu.VMEM((HD, cols), jnp.bfloat16),
            pltpu.VMEM((HD, cols), jnp.float32),
        ],
        compiler_params=pltpu.CompilerParams(vmem_limit_bytes=VMEM_BYTES),
    )(doc_starts, assign, queries, d_out, kv_all)


def body(queries, keys, values, d_out, doc_starts, assign):
    tokens = assign.shape[0] * SPAN
    dims = tuple(SIZES[axis] for axis in AXES)
    kv_all = gather_all(keys, values).reshape(2, tokens, HD)
    attn_out, d_query, terms = attention(doc_starts, assign, queries, d_out, kv_all)
    summed = reduce_all(terms.reshape(2, *dims, ROWS, HD))
    return (attn_out, d_query, summed[0], summed[1])


def solution(mesh):
    placed = (P("ctx", "head"), P("ctx", None), P("ctx", None), P("ctx", "head"), P(), P())
    return jax.shard_map(
        body,
        mesh=mesh,
        in_specs=placed,
        out_specs=(P("ctx", "head"), P("ctx", "head"), P("ctx", None), P("ctx", None)),
        check_vma=False,
    )
```

```python
import math

import jax
import jax.numpy as jnp
from jax import lax
from jax.experimental import pallas as pl
from jax.experimental.pallas import tpu as pltpu
from jax.sharding import PartitionSpec as P

HD = 128
SPAN = 64
ROWS = 2 * SPAN
BLOCK = 512
UNIT = 512
MESH = pl.DeviceIdType.MESH
AXES = ("z", "y", "x")
SIZES = {"z": 8, "y": 4, "x": 4}
ROUTE_A = (0, 32)
ROUTES = ((32, 48, "y", "x"), (80, 48, "x", "y"))
NEAR = (1, -1, 2)
Z_AWAY = (1, -1, 2, -2, 3, -3, 4)
GROUPS = ((0,), (1, -1), (2, -2), (3, -3), (4,))
DIRECT = (4,)
SUM_DIRECT = (0,)
COPIES = 80
ZERO_PIECES = 8
VMEM_BYTES = 60 * 1024 * 1024


def my_place():
    me = lax.axis_index("ctx")
    nx, ny = SIZES["x"], SIZES["y"]
    pos = {"x": lax.rem(me, nx), "y": lax.rem(me // nx, ny), "z": me // (nx * ny)}
    return pos, me, lax.axis_index("head")


def wrapped(value, size):
    return lax.rem(value + 2 * size, size)


def shifted(pos, axis, step):
    return wrapped(pos[axis] + step, SIZES[axis])


def peer(pos, core, axis, step):
    there = dict(pos)
    there[axis] = shifted(pos, axis, step)
    return ((there["z"] * SIZES["y"] + there["y"]) * SIZES["x"] + there["x"], core)


def greet(pos, me, core, along_z):
    barrier = pltpu.get_barrier_semaphore()
    partners = [("z", step) for step in along_z] + [(axis, step) for axis in "yx" for step in NEAR]
    for axis, step in partners:
        pl.semaphore_signal(
            barrier, inc=1, device_id=peer(pos, core, axis, step), device_id_type=MESH
        )
    pl.semaphore_signal(barrier, inc=1, device_id=(me, 1 - core), device_id_type=MESH)
    pl.semaphore_wait(barrier, len(partners) + 1)


def as_f32(value):
    return value.astype(jnp.float32)


class Numbers(dict):
    def __missing__(self, key):
        self[key] = len(self)
        assert len(self) <= COPIES
        return self[key]


def gather_kernel(
    k_ref, v_ref, all_ref, zeros_ref, recv, send_sem, side_send, side_recv, own_sem, zero_sem, blank
):
    pos, me, core = my_place()
    here = tuple(pl.ds(pos[axis], 1) for axis in AXES)
    for which, ref in ((0, k_ref), (1, v_ref)):
        @pl.when(core == which)
        def _(ref=ref):
            pltpu.make_async_copy(ref, all_ref.at[(core, *here)], own_sem).start()
    greet(pos, me, core, (1, -1))

    number = Numbers()
    sent_rows = []

    def view(owner, rows, **sel):
        index = [sel[axis] if axis in sel else (pos[axis], 1) for axis in AXES]
        return all_ref.at[(owner, *(pl.ds(*at) for at in index), pl.ds(*rows), slice(None))]

    def push(key, axis, step, rows, sel, src=None):
        ref = view(core, rows, **sel)
        pltpu.make_async_remote_copy(
            src_ref=ref if src is None else src.at[:, :, :, pl.ds(*rows), :],
            dst_ref=ref, send_sem=send_sem, recv_sem=recv.at[number[key]],
            device_id=peer(pos, core, axis, step), device_id_type=MESH,
        ).start()
        sent_rows.append(rows[1] * math.prod(count for _, count in sel.values()))

    def arrive(key, rows, sel):
        ref = view(core, rows, **sel)
        pltpu.make_async_remote_copy(
            src_ref=ref, dst_ref=ref, send_sem=send_sem, recv_sem=recv.at[number[key]],
            device_id=(me, 1 - core), device_id_type=MESH,
        ).wait_recv()

    def side(ref):
        return pltpu.make_async_remote_copy(
            src_ref=ref, dst_ref=ref, send_sem=side_send, recv_sem=side_recv,
            device_id=(me, 1 - core), device_id_type=MESH,
        )

    def hand_over(rows, **sel):
        side(view(core, rows, **sel)).start()

    def full(axis):
        return (0, SIZES[axis])

    def half(axis, side_at):
        return (side_at * (SIZES[axis] // 2), SIZES[axis] // 2)

    def z_way(route, d):
        if d == 4:
            return 1 - 2 * route
        return -1 if d > 0 else 1

    def at_z(d):
        return (shifted(pos, "z", d), 1)

    def to_z(route, d, src=None):
        first, count, _, _ = ROUTES[route]
        toward = z_way(route, d)
        push(("z", route, d), "z", toward, (first, count), {"z": at_z(d + toward)}, src)

    def from_z(route, d):
        first, count, _, _ = ROUTES[route]
        arrive(("z", route, d), (first, count), {"z": at_z(d)})
        if abs(d) < 3:
            to_z(route, d - z_way(route, d))
        elif d != 4 and z_way(route, d) == z_way(route, 4):
            to_z(route, 4)

    def to_middle(route, d, src=None):
        first, count, middle, _ = ROUTES[route]
        for m in NEAR:
            push(("m", route, d), middle, m, (first, count), {"z": at_z(d)}, src)

    def from_middle(route, d):
        first, count, middle, _ = ROUTES[route]
        arrive(("m", route, d), (first, count), {"z": at_z(d), middle: (0, len(NEAR))})

    def to_last(route, d):
        first, count, middle, last = ROUTES[route]
        sel = {"z": at_z(d), middle: full(middle)}
        for m in (NEAR if d in DIRECT else NEAR[:2]):
            push(("l", route, d), last, m, (first, count), sel)

    def whole_plane(route, d):
        first, count, _, _ = ROUTES[route]
        hand_over((first, count), z=at_z(d), y=full("y"), x=full("x"))

    def pass_last(route, d):
        first, count, middle, last = ROUTES[route]
        copies = len(NEAR) if d in DIRECT else 2
        arrive(("l", route, d), (first, count), {"z": at_z(d), middle: full(middle), last: (0, copies)})
        if d in DIRECT:
            whole_plane(route, d)
            return
        for way, m in enumerate(NEAR[:2]):
            sel = {"z": at_z(d), middle: half(middle, way), last: (shifted(pos, last, -m), 1)}
            push(("p", route, d), last, m, (first, count), sel)

    def from_last(route, d):
        first, count, middle, last = ROUTES[route]
        if d in DIRECT:
            return
        arrive(("p", route, d), (first, count), {"z": at_z(d), middle: full(middle)})
        whole_plane(route, d)

    def ring_sel(part, step, way, arriving):
        toward = 1 - 2 * way
        back = step if arriving else step - 1
        sel = {"z": (shifted(pos, "z", -toward * back), 1), "y": half("y", part), "x": full("x")}
        if step == SIZES["z"] // 2:
            sel["x"] = half("x", way)
        return sel

    def a_ring(step):
        steps = SIZES["z"] // 2
        for part in (0, 1):
            for way in (0, 1):
                if step > 1:
                    arrive(("r", part, step - 1, way), ROUTE_A, ring_sel(part, step - 1, way, True))
                if step <= steps:
                    push(("r", part, step, way), "z", 1 - 2 * way, ROUTE_A, ring_sel(part, step, way, False))
        for d in {1: (0,), steps + 1: (steps,)}.get(step, (step - 1, 1 - step)):
            hand_over(ROUTE_A, z=at_z(d), y=full("y"), x=full("x"))

    both = range(len(ROUTES))

    def begin(src):
        for route in both:
            for d in GROUPS[1]:
                to_z(route, d, src)
        for route in both:
            to_middle(route, 0, src)
        for m in NEAR:
            push(("y",), "y", m, ROUTE_A, {}, src)

    for which, ref in ((0, k_ref), (1, v_ref)):
        @pl.when(core == which)
        def _(ref=ref):
            sent_rows.clear()
            begin(ref)
    pltpu.make_async_copy(k_ref, all_ref.at[(core, *here)], own_sem).wait()
    blank[...] = jnp.zeros_like(blank)
    piece = blank.shape[0]
    pieces = zeros_ref.shape[0] // piece

    def wipe(at):
        return pltpu.make_async_copy(blank, zeros_ref.at[pl.ds(at * piece, piece)], zero_sem.at[at])

    for at in range(len(GROUPS) + 2):
        if at + 1 < len(GROUPS):
            for route in both:
                for d in GROUPS[at + 1]:
                    from_z(route, d)
                    to_middle(route, d)
        if at < len(GROUPS):
            for route in both:
                for d in GROUPS[at]:
                    from_middle(route, d)
                    to_last(route, d)
        if at == 0:
            arrive(("y",), ROUTE_A, {"y": (0, len(NEAR))})
            for m in NEAR:
                push(("x",), "x", m, ROUTE_A, {"y": full("y")})
        if at == 1:
            arrive(("x",), ROUTE_A, {"y": full("y"), "x": (0, len(NEAR))})
        if 0 < at <= SIZES["z"] // 2 + 1:
            a_ring(at)
        if 0 < at <= len(GROUPS):
            for route in both:
                for d in GROUPS[at - 1]:
                    pass_last(route, d)
        if 1 < at:
            for route in both:
                for d in GROUPS[at - 2]:
                    from_last(route, d)
        for i in range(at * 2, min(at * 2 + 2, pieces)):
            wipe(i).start()
    for at in range(pieces):
        wipe(at).wait()
    sent = zeros_ref.at[pl.ds(0, sum(sent_rows))]
    pltpu.make_async_remote_copy(
        src_ref=sent, dst_ref=sent, send_sem=send_sem, recv_sem=side_recv,
        device_id=(me, 1 - core), device_id_type=MESH,
    ).wait_send()
    side(all_ref.at[core]).wait_send()
    side(all_ref.at[1 - core]).wait_recv()


def gather_all(keys, values):
    dims = tuple(SIZES[axis] for axis in AXES)
    sems = pltpu.SemaphoreType.DMA((COPIES,))
    one_sem = pltpu.SemaphoreType.DMA
    piece = 2 * math.prod(dims) * ROWS // ZERO_PIECES
    anywhere = pl.BlockSpec(memory_space=pl.ANY)
    return pl.pallas_call(
        gather_kernel,
        out_shape=(
            jax.ShapeDtypeStruct((2, *dims, ROWS, HD), jnp.bfloat16),
            jax.ShapeDtypeStruct((ZERO_PIECES * piece, HD), jnp.bfloat16),
        ),
        in_specs=[anywhere, anywhere],
        out_specs=(anywhere, anywhere),
        scratch_shapes=[sems, one_sem, one_sem, one_sem, one_sem,
                        pltpu.SemaphoreType.DMA((ZERO_PIECES,)), pltpu.VMEM((piece, HD), jnp.bfloat16)],
        compiler_params=pltpu.CompilerParams(
            collective_id=0, has_side_effects=True, vmem_limit_bytes=VMEM_BYTES
        ),
    )(keys.reshape(1, 1, 1, ROWS, HD), values.reshape(1, 1, 1, ROWS, HD))


def reduce_kernel(
    terms_ref, out_ref, held, other, final, ring_land, ax_land, ay_land, first_land, second_land,
    direct_land, middle_land, z_land, send, recv, load_sem, side_send, side_recv, last_send, last_recv,
):
    pos, me, core = my_place()
    sibling = (me, 1 - core)

    def load(d):
        z = shifted(pos, "z", d)
        return pltpu.make_async_copy(terms_ref.at[core, z], held.at[z], load_sem.at[d % 8])

    def side(d):
        z = shifted(pos, "z", d)
        return pltpu.make_async_remote_copy(
            src_ref=terms_ref.at[1 - core, z], dst_ref=other.at[z],
            send_sem=side_send, recv_sem=side_recv.at[d % 8],
            device_id=sibling, device_id_type=MESH,
        )

    far_first = GROUPS[::-1]
    for group in far_first:
        for d in group:
            load(d).start()
    greet(pos, me, core, Z_AWAY)
    for group in far_first:
        for d in group:
            side(d).start()

    number, kind = Numbers(), Numbers()

    def copy(key, axis, step, src, dst):
        return pltpu.make_async_remote_copy(
            src_ref=src, dst_ref=dst, send_sem=send.at[kind[key[0]]], recv_sem=recv.at[number[key]],
            device_id=peer(pos, core, axis, step), device_id_type=MESH,
        )

    def push(*item):
        copy(*item).start()

    def arrived(key, land):
        copy(key, "z", 1, land, land).wait_recv()

    def left(name, land):
        copy((name,), "z", 1, land, land).wait_send()

    def held_at(rows, **sel):
        index = []
        for axis in AXES:
            at = sel[axis] if axis in sel else pos[axis]
            index.append(pl.ds(*at) if isinstance(at, tuple) else at)
        return (*index, pl.ds(*rows), slice(None))

    def add(where, lands):
        total = as_f32(held[where])
        for land in lands:
            total = total + as_f32(land[...])
        held[where] = total.astype(jnp.bfloat16)

    def join(d):
        load(d).wait()
        side(d).wait_recv()
        z = shifted(pos, "z", d)

        def one(y, carry):
            for x in range(SIZES["x"]):
                held[z, y, x] = (as_f32(held[z, y, x]) + as_f32(other[z, y, x])).astype(jnp.bfloat16)
            return carry

        lax.fori_loop(0, SIZES["y"], one, 0)

    def middle_half(middle, way):
        size = SIZES[middle] // 2
        return (way * size, size)

    def first_copy(route, d, way):
        first, count, middle, last = ROUTES[route]
        where = {"z": shifted(pos, "z", d), middle: middle_half(middle, way), last: shifted(pos, last, 2)}
        return (("f", route, d), last, 1 - 2 * way, held.at[held_at((first, count), **where)],
                first_land.at[route, d % 8, way])

    def second_copy(route, d, way):
        first, count, middle, last = ROUTES[route]
        where = {"z": shifted(pos, "z", d), middle: (0, SIZES[middle]), last: shifted(pos, last, 1 - 2 * way)}
        return (("s", route, d), last, 1 - 2 * way, held.at[held_at((first, count), **where)],
                second_land.at[route, d % 8, way])

    def middle_copy(route, d, m):
        first, count, middle, last = ROUTES[route]
        where = {"z": shifted(pos, "z", d), middle: shifted(pos, middle, m)}
        return (("m", route, d), middle, m, held.at[held_at((first, count), **where)],
                middle_land.at[route, d % 8, NEAR.index(m)])

    def z_copy(route, d):
        first, count, _, _ = ROUTES[route]
        return (("z", route), "z", d, held.at[held_at((first, count), z=shifted(pos, "z", d))],
                z_land.at[route, Z_AWAY.index(d)])

    def direct_copy(route, d, m):
        first, count, middle, last = ROUTES[route]
        where = {"z": shifted(pos, "z", d), middle: (0, SIZES[middle]), last: shifted(pos, last, m)}
        return (("d", route, d), last, m, held.at[held_at((first, count), **where)],
                direct_land.at[route, SUM_DIRECT.index(d), NEAR.index(m)])

    def send_first(route, d):
        if d in SUM_DIRECT:
            for m in NEAR:
                push(*direct_copy(route, d, m))
            return
        for way in (0, 1):
            push(*first_copy(route, d, way))

    def send_second(route, d):
        first, count, middle, last = ROUTES[route]
        arrived(("f", route, d), first_land.at[route, d % 8])
        for way in (0, 1):
            low, size = middle_half(middle, way)
            for i in range(size):
                where = {"z": shifted(pos, "z", d), middle: low + i, last: shifted(pos, last, 1 - 2 * way)}
                add(held_at((first, count), **where), [first_land.at[route, d % 8, way, i]])
            push(*second_copy(route, d, way))

    def send_middle(route, d):
        first, count, middle, last = ROUTES[route]
        if d in SUM_DIRECT:
            arrived(("d", route, d), direct_land.at[route, SUM_DIRECT.index(d)])
            lands = [direct_land.at[route, SUM_DIRECT.index(d), i] for i in range(len(NEAR))]
        else:
            arrived(("s", route, d), second_land.at[route, d % 8])
            lands = [second_land.at[route, d % 8, way] for way in (0, 1)]
        for i in range(SIZES[middle]):
            where = {"z": shifted(pos, "z", d), middle: i}
            add(held_at((first, count), **where), [land.at[i] for land in lands])
        for m in NEAR:
            push(*middle_copy(route, d, m))

    def send_z(route, d):
        first, count, _, _ = ROUTES[route]
        arrived(("m", route, d), middle_land.at[route, d % 8])
        where = held_at((first, count), z=shifted(pos, "z", d))
        add(where, [middle_land.at[route, d % 8, i] for i in range(len(NEAR))])
        if d != 0:
            push(*z_copy(route, d))

    def ring_copy(step, way):
        toward = 1 - 2 * way
        half = SIZES["x"] // 2
        xs = (way * half, half) if step == 1 else (0, SIZES["x"])
        where = {"z": shifted(pos, "z", toward * (5 - step)), "y": (0, SIZES["y"]), "x": xs}
        return (("h" if step == 1 else "r", step, way), "z", toward, held.at[held_at(ROUTE_A, **where)],
                ring_land.at[way, step - 1, :, pl.ds(*xs)])

    def ring(step):
        for way in (0, 1):
            toward = 1 - 2 * way
            half = SIZES["x"] // 2
            if 1 < step < 5:
                copy(*ring_copy(step - 1, way)).wait_recv()
                low, size = (way * half, half) if step == 2 else (0, SIZES["x"])
                z = shifted(pos, "z", toward * (5 - step))

                def one(y, carry):
                    for i in range(size):
                        add(held_at(ROUTE_A, z=z, y=y, x=low + i), [ring_land.at[way, step - 2, y, low + i]])
                    return carry

                lax.fori_loop(0, SIZES["y"], one, 0)
            if step < 5:
                push(*ring_copy(step, way))
        if step == 5:
            for way in (0, 1):
                copy(*ring_copy(4, way)).wait_recv()

            def last(y, carry):
                for x in range(SIZES["x"]):
                    add(held_at(ROUTE_A, y=y, x=x), [ring_land.at[way, 3, y, x] for way in (0, 1)])
                return carry

            lax.fori_loop(0, SIZES["y"], last, 0)

    def ax_copy(m):
        where = {"y": (0, SIZES["y"]), "x": shifted(pos, "x", m)}
        return (("ax",), "x", m, held.at[held_at(ROUTE_A, **where)], ax_land.at[NEAR.index(m)])

    def ay_copy(m):
        where = {"y": shifted(pos, "y", m)}
        return (("ay",), "y", m, held.at[held_at(ROUTE_A, **where)], ay_land.at[NEAR.index(m)])

    both = range(len(ROUTES))
    for at in range(len(far_first) + 2):
        if at < len(far_first):
            for d in far_first[at]:
                join(d)
            for route in both:
                for d in far_first[at]:
                    send_first(route, d)
            ring(at + 1)
        if at == len(far_first) - 1:
            for m in NEAR:
                push(*ax_copy(m))
        for behind, act in ((1, send_second), (2, send_middle), (3, send_z)):
            for begun, group in enumerate(far_first):
                for d in group:
                    sooner = 1 if d in SUM_DIRECT else 0
                    if begun + behind - sooner == at and not (sooner and act is send_second):
                        for route in both:
                            act(route, d)
        if at == len(far_first):
            arrived(("ax",), ax_land)
            for y in range(SIZES["y"]):
                add(held_at(ROUTE_A, y=y), [ax_land.at[i, y] for i in range(len(NEAR))])
            for m in NEAR:
                push(*ay_copy(m))
    arrived(("ay",), ay_land)
    add(held_at(ROUTE_A), [ay_land.at[i] for i in range(len(NEAR))])
    for route in both:
        first, count, _, _ = ROUTES[route]
        arrived(("z", route), z_land.at[route])
        add(held_at((first, count)), [z_land.at[route, i] for i in range(len(Z_AWAY))])

    final[core] = held[pos["z"], pos["y"], pos["x"]]
    last_copy = pltpu.make_async_remote_copy(
        src_ref=final.at[core], dst_ref=final.at[core], send_sem=last_send, recv_sem=last_recv,
        device_id=sibling, device_id_type=MESH,
    )
    last_copy.start()
    pltpu.make_async_remote_copy(
        src_ref=other, dst_ref=other, send_sem=side_send, recv_sem=last_recv,
        device_id=sibling, device_id_type=MESH,
    ).wait_send()
    relayed = pl.ds(0, SIZES["z"] - len(SUM_DIRECT))
    left("f", first_land.at[:, relayed])
    left("s", second_land.at[:, relayed])
    left("d", direct_land)
    left("m", middle_land)
    left("z", z_land)
    left("h", ring_land.at[:, 0, :, pl.ds(0, SIZES["x"] // 2)])
    left("r", ring_land.at[:, pl.ds(1, 3)])
    left("ax", ax_land)
    left("ay", ay_land)
    last_copy.wait()
    out_ref[...] = final[...]


def reduce_all(terms):
    dims = tuple(SIZES[axis] for axis in AXES)
    nz, ny, nx = dims

    def vmem(*shape):
        return pltpu.VMEM((*shape, HD), jnp.bfloat16)

    count = ROUTES[0][1]
    routes = len(ROUTES)
    sems = pltpu.SemaphoreType.DMA((COPIES,))
    by_z = pltpu.SemaphoreType.DMA((nz,))
    one_sem = pltpu.SemaphoreType.DMA
    return pl.pallas_call(
        reduce_kernel,
        out_shape=jax.ShapeDtypeStruct((2, ROWS, HD), jnp.bfloat16),
        in_specs=[pl.BlockSpec(memory_space=pl.ANY)],
        out_specs=pl.BlockSpec(memory_space=pltpu.VMEM),
        scratch_shapes=[
            vmem(*dims, ROWS),
            vmem(*dims, ROWS),
            vmem(2, ROWS),
            vmem(2, nz // 2, ny, nx, ROUTE_A[1]),
            vmem(len(NEAR), ny, ROUTE_A[1]),
            vmem(len(NEAR), ROUTE_A[1]),
            vmem(routes, nz, 2, 2, count),
            vmem(routes, nz, 2, 4, count),
            vmem(routes, len(SUM_DIRECT), len(NEAR), 4, count),
            vmem(routes, nz, len(NEAR), count),
            vmem(routes, len(Z_AWAY), count),
            pltpu.SemaphoreType.DMA((9,)), sems, by_z, one_sem, by_z, one_sem, one_sem,
        ],
        compiler_params=pltpu.CompilerParams(
            collective_id=1, has_side_effects=True, vmem_limit_bytes=VMEM_BYTES
        ),
    )(terms)


def dot(left, right, contract):
    return lax.dot_general(
        left, right, ((contract[:1], contract[1:]), ((), ())), preferred_element_type=jnp.float32
    )


def attention_kernel(
    starts_ref, assign_ref, q_ref, g_ref, kv_ref, zeros_ref, out_ref, dq_ref, terms_ref,
    place_ref, tiles, sums, scores, probs, q_cols, g_cols, acc, in_sem, out_sem,
):
    del zeros_ref
    heads = q_ref.shape[1] // HD
    cols = heads * SPAN
    scale = 1.0 / math.sqrt(HD)
    to_exp2 = scale * math.log2(math.e)
    per_block = BLOCK // SPAN

    def locate(at, carry):
        for i in range(16):
            place_ref[assign_ref[at * 16 + i]] = at * 16 + i
        return carry

    lax.fori_loop(0, assign_ref.shape[0] // 16, locate, 0)
    first_span = lax.axis_index("ctx") * 2
    bases, firsts, lasts = [], [], []
    for part in range(2):
        base = assign_ref[first_span + part] * SPAN
        doc_first = jnp.int32(0)
        for doc in range(starts_ref.shape[0]):
            start = starts_ref[doc]
            doc_first = jnp.where(start <= base, jnp.maximum(doc_first, start), doc_first)
        bases.append(base)
        firsts.append(doc_first // BLOCK)
        lasts.append(base // BLOCK)

    def rows_at(at, count):
        return pl.ds(pl.multiple_of(at * count, count), count)

    def stored(block, i):
        return rows_at(place_ref[block * per_block + i], SPAN)

    def fetch(part, at):
        for i in range(per_block):
            pltpu.make_async_copy(
                kv_ref.at[:, stored(firsts[part] + at, i), :],
                tiles.at[part, :, rows_at(at * per_block + i, SPAN), :],
                in_sem.at[part, at],
            ).start()

    def fetched(part, at):
        pltpu.make_async_copy(
            kv_ref.at[:, pl.ds(0, BLOCK), :], tiles.at[part, :, rows_at(at, BLOCK), :], in_sem.at[part, at]
        ).wait()

    def store(block):
        for i in range(per_block):
            pltpu.make_async_copy(
                sums.at[:, rows_at(block * per_block + i, SPAN), :],
                terms_ref.at[:, stored(block, i), :],
                out_sem.at[block],
            ).start()

    def stored_all(block):
        pltpu.make_async_copy(
            sums.at[:, rows_at(block, BLOCK), :], terms_ref.at[:, pl.ds(0, BLOCK), :], out_sem.at[block]
        ).wait()

    def shared(block):
        return (block >= firsts[1]) & (block <= lasts[1])

    for part in range(2):
        lax.fori_loop(0, lasts[part] - firsts[part] + 1, lambda at, c, part=part: (fetch(part, at), c)[1], 0)

    for part in range(2):
        base = bases[part]
        full_blocks = lasts[part] - firsts[part]
        inside = base - lasts[part] * BLOCK

        rows = pl.ds(part * SPAN, SPAN)
        q_rows = jnp.concatenate(
            [q_ref[rows, h * HD : (h + 1) * HD] for h in range(heads)], axis=0
        )
        g_rows = jnp.concatenate(
            [g_ref[rows, h * HD : (h + 1) * HD] for h in range(heads)], axis=0
        )
        q_t = as_f32(q_rows).T
        g_t = as_f32(g_rows).T
        q_cols[...] = q_t.astype(jnp.bfloat16)
        g_cols[...] = g_t.astype(jnp.bfloat16)

        def tile(which, at, part=part):
            return tiles[part, which, rows_at(at, BLOCK), :]

        def fold(value, op):
            value = value.reshape(BLOCK // 8, 8, cols)
            return op(value, axis=0)

        def score_step(at, top, part=part):
            fetched(part, at)
            s = dot(tile(0, at), q_cols[...], (1, 0))
            scores[at] = s
            return jnp.maximum(top, fold(s, jnp.max))

        top = lax.fori_loop(0, full_blocks, score_step, jnp.full((8, cols), -1e30, jnp.float32))
        fetched(part, full_blocks)
        s = dot(tile(0, full_blocks), q_cols[...], (1, 0))
        key_at = lax.broadcasted_iota(jnp.int32, (BLOCK, cols), 0)
        query_at = lax.broadcasted_iota(jnp.int32, (BLOCK, cols), 1)
        s = jnp.where(key_at <= inside + lax.rem(query_at, SPAN), s, -1e30)
        scores[full_blocks] = s
        top = jnp.max(jnp.maximum(top, fold(s, jnp.max)), axis=0, keepdims=True)

        acc[...] = jnp.zeros_like(acc)

        def value_step(at, total):
            p = jnp.exp2((scores[at] - top) * to_exp2)
            p16 = p.astype(jnp.bfloat16)
            probs[at] = p16
            acc[...] += dot(tile(1, at), p16, (0, 0))
            return total + fold(p, jnp.sum)

        total = lax.fori_loop(0, full_blocks + 1, value_step, jnp.zeros((8, cols), jnp.float32))
        inverse = 1.0 / jnp.sum(total, axis=0, keepdims=True)
        out_t = (acc[...] * inverse).astype(jnp.bfloat16).astype(jnp.float32)
        delta = jnp.sum(g_t * out_t, axis=0, keepdims=True)
        q_scaled = (q_t * (inverse * scale)).astype(jnp.bfloat16)
        g_scaled = (g_t * inverse).astype(jnp.bfloat16)
        out_rows = out_t.T.astype(jnp.bfloat16)
        acc[...] = jnp.zeros_like(acc)

        def grad_step(at, carry, part=part):
            block = firsts[part] + at
            p16 = probs[at]
            keys = tile(0, at)
            d_probs = dot(tile(1, at), g_cols[...], (1, 0))
            d_scores = (as_f32(p16) * (d_probs - delta)).astype(jnp.bfloat16)
            acc[...] += dot(keys, d_scores, (0, 0))
            d_key = dot(d_scores, q_scaled, (1, 1))
            d_value = dot(p16, g_scaled, (1, 1))
            here = rows_at(block, BLOCK)
            for which, term in ((0, d_key), (1, d_value)):
                if part > 0:
                    both = (block >= firsts[0]) & (block <= lasts[0])
                    term = term + jnp.where(both, as_f32(sums[which, here, :]), 0.0)
                sums[which, here, :] = term.astype(jnp.bfloat16)
            if part > 0:
                store(block)
            else:
                pl.when(jnp.logical_not(shared(block)))(lambda: store(block))
            return carry

        lax.fori_loop(0, full_blocks + 1, grad_step, 0)
        dq_rows = (acc[...] * (inverse * scale)).T.astype(jnp.bfloat16)
        for h in range(heads):
            out_ref[rows, h * HD : (h + 1) * HD] = out_rows[h * SPAN : (h + 1) * SPAN]
            dq_ref[rows, h * HD : (h + 1) * HD] = dq_rows[h * SPAN : (h + 1) * SPAN]

    def drain(block, carry, part):
        if part > 0:
            stored_all(block)
        else:
            pl.when(jnp.logical_not(shared(block)))(lambda: stored_all(block))
        return carry

    for part in range(2):
        lax.fori_loop(firsts[part], lasts[part] + 1, lambda block, c, part=part: drain(block, c, part), 0)


def attention(doc_starts, assign, queries, d_out, kv_all, zeros):
    tokens = kv_all.shape[1]
    heads = queries.shape[1] // HD
    cols = heads * SPAN
    longest = tokens - (doc_starts.shape[0] - 1) * UNIT
    blocks = -(-longest // BLOCK)
    smem = pl.BlockSpec(memory_space=pltpu.SMEM)
    vmem = pl.BlockSpec(memory_space=pltpu.VMEM)
    anywhere = pl.BlockSpec(memory_space=pl.ANY)
    return pl.pallas_call(
        attention_kernel,
        out_shape=(
            jax.ShapeDtypeStruct(queries.shape, jnp.bfloat16),
            jax.ShapeDtypeStruct(queries.shape, jnp.bfloat16),
            jax.ShapeDtypeStruct(zeros.shape, jnp.bfloat16),
        ),
        in_specs=[smem, smem, vmem, vmem, anywhere, anywhere],
        out_specs=(vmem, vmem, anywhere),
        input_output_aliases={5: 2},
        scratch_shapes=[
            pltpu.SMEM(assign.shape, jnp.int32),
            pltpu.VMEM((2, 2, blocks * BLOCK, HD), jnp.bfloat16),
            pltpu.VMEM((2, tokens, HD), jnp.bfloat16),
            pltpu.VMEM((blocks, BLOCK, cols), jnp.float32),
            pltpu.VMEM((blocks, BLOCK, cols), jnp.bfloat16),
            pltpu.VMEM((HD, cols), jnp.bfloat16),
            pltpu.VMEM((HD, cols), jnp.bfloat16),
            pltpu.VMEM((HD, cols), jnp.float32),
            pltpu.SemaphoreType.DMA((2, blocks)),
            pltpu.SemaphoreType.DMA((tokens // BLOCK,)),
        ],
        compiler_params=pltpu.CompilerParams(vmem_limit_bytes=VMEM_BYTES),
    )(doc_starts, assign, queries, d_out, kv_all, zeros)


def body(queries, keys, values, d_out, doc_starts, assign):
    tokens = assign.shape[0] * SPAN
    dims = tuple(SIZES[axis] for axis in AXES)
    kv_all, zeros = gather_all(keys, values)
    attn_out, d_query, terms = attention(
        doc_starts, assign, queries, d_out, kv_all.reshape(2, tokens, HD), zeros.reshape(2, tokens, HD)
    )
    summed = reduce_all(terms.reshape(2, *dims, ROWS, HD))
    return (attn_out, d_query, summed[0], summed[1])


def solution(mesh):
    placed = (P("ctx", "head"), P("ctx", None), P("ctx", None), P("ctx", "head"), P(), P())
    return jax.shard_map(
        body,
        mesh=mesh,
        in_specs=placed,
        out_specs=(P("ctx", "head"), P("ctx", "head"), P("ctx", None), P("ctx", None)),
        check_vma=False,
    )
```

```python
import math

import jax
import jax.numpy as jnp
from jax import lax
from jax.experimental import pallas as pl
from jax.experimental.pallas import tpu as pltpu
from jax.sharding import PartitionSpec as P

HD = 128
SPAN = 64
ROWS = 2 * SPAN
BLOCK = 512
UNIT = 512
STEPS = (4, 2, 1)
MESH = pl.DeviceIdType.MESH
AXES = ("z", "y", "x")
SIZES = {"z": 8, "y": 4, "x": 4}
ROUTE_A = (0, 32)
ROUTES = ((32, 48, "y", "x"), (80, 48, "x", "y"))
NEAR = (1, -1, 2)
Z_AWAY = (1, -1, 2, -2, 3, -3, 4)
GROUPS = ((0,), (1, -1), (2, -2), (3, -3), (4,))
DIRECT = (4, 3, -3)
SUM_DIRECT = (0, 1, -1)
COPIES = 80
ZERO_PIECES = 8
VMEM_BYTES = 60 * 1024 * 1024


def my_place():
    me = lax.axis_index("ctx")
    nx, ny = SIZES["x"], SIZES["y"]
    pos = {"x": lax.rem(me, nx), "y": lax.rem(me // nx, ny), "z": me // (nx * ny)}
    return pos, me, lax.axis_index("head")


def wrapped(value, size):
    return lax.rem(value + 2 * size, size)


def shifted(pos, axis, step):
    return wrapped(pos[axis] + step, SIZES[axis])


def peer(pos, core, axis, step):
    there = dict(pos)
    there[axis] = shifted(pos, axis, step)
    return ((there["z"] * SIZES["y"] + there["y"]) * SIZES["x"] + there["x"], core)


def greet(pos, me, core, along_z):
    barrier = pltpu.get_barrier_semaphore()
    partners = [("z", step) for step in along_z] + [(axis, step) for axis in "yx" for step in NEAR]
    for axis, step in partners:
        pl.semaphore_signal(
            barrier, inc=1, device_id=peer(pos, core, axis, step), device_id_type=MESH
        )
    pl.semaphore_signal(barrier, inc=1, device_id=(me, 1 - core), device_id_type=MESH)
    pl.semaphore_wait(barrier, len(partners) + 1)


def as_f32(value):
    return value.astype(jnp.float32)


class Numbers(dict):
    def __missing__(self, key):
        self[key] = len(self)
        assert len(self) <= COPIES
        return self[key]


def gather_kernel(
    k_ref, v_ref, all_ref, zeros_ref, recv, send_sem, side_send, side_recv, own_sem, zero_sem, blank
):
    pos, me, core = my_place()
    here = tuple(pl.ds(pos[axis], 1) for axis in AXES)
    for which, ref in ((0, k_ref), (1, v_ref)):
        @pl.when(core == which)
        def _(ref=ref):
            pltpu.make_async_copy(ref, all_ref.at[(core, *here)], own_sem).start()
    greet(pos, me, core, (1, -1))

    number = Numbers()
    sent_rows = []

    def view(owner, rows, **sel):
        index = [sel[axis] if axis in sel else (pos[axis], 1) for axis in AXES]
        return all_ref.at[(owner, *(pl.ds(*at) for at in index), pl.ds(*rows), slice(None))]

    def push(key, axis, step, rows, sel, src=None):
        ref = view(core, rows, **sel)
        pltpu.make_async_remote_copy(
            src_ref=ref if src is None else src.at[:, :, :, pl.ds(*rows), :],
            dst_ref=ref, send_sem=send_sem, recv_sem=recv.at[number[key]],
            device_id=peer(pos, core, axis, step), device_id_type=MESH,
        ).start()
        sent_rows.append(rows[1] * math.prod(count for _, count in sel.values()))

    def arrive(key, rows, sel):
        ref = view(core, rows, **sel)
        pltpu.make_async_remote_copy(
            src_ref=ref, dst_ref=ref, send_sem=send_sem, recv_sem=recv.at[number[key]],
            device_id=(me, 1 - core), device_id_type=MESH,
        ).wait_recv()

    def side(ref):
        return pltpu.make_async_remote_copy(
            src_ref=ref, dst_ref=ref, send_sem=side_send, recv_sem=side_recv,
            device_id=(me, 1 - core), device_id_type=MESH,
        )

    def hand_over(rows, **sel):
        side(view(core, rows, **sel)).start()

    def full(axis):
        return (0, SIZES[axis])

    def half(axis, side_at):
        return (side_at * (SIZES[axis] // 2), SIZES[axis] // 2)

    def z_way(route, d):
        if d == 4:
            return 1 - 2 * route
        return -1 if d > 0 else 1

    def at_z(d):
        return (shifted(pos, "z", d), 1)

    def to_z(route, d, src=None):
        first, count, _, _ = ROUTES[route]
        toward = z_way(route, d)
        push(("z", route, d), "z", toward, (first, count), {"z": at_z(d + toward)}, src)

    def from_z(route, d):
        first, count, _, _ = ROUTES[route]
        arrive(("z", route, d), (first, count), {"z": at_z(d)})
        if abs(d) < 3:
            to_z(route, d - z_way(route, d))
        elif d != 4 and z_way(route, d) == z_way(route, 4):
            to_z(route, 4)

    def to_middle(route, d, src=None):
        first, count, middle, _ = ROUTES[route]
        for m in NEAR:
            push(("m", route, d), middle, m, (first, count), {"z": at_z(d)}, src)

    def from_middle(route, d):
        first, count, middle, _ = ROUTES[route]
        arrive(("m", route, d), (first, count), {"z": at_z(d), middle: (0, len(NEAR))})

    def to_last(route, d):
        first, count, middle, last = ROUTES[route]
        sel = {"z": at_z(d), middle: full(middle)}
        for m in (NEAR if d in DIRECT else NEAR[:2]):
            push(("l", route, d), last, m, (first, count), sel)

    def whole_plane(route, d):
        first, count, _, _ = ROUTES[route]
        hand_over((first, count), z=at_z(d), y=full("y"), x=full("x"))

    def pass_last(route, d):
        first, count, middle, last = ROUTES[route]
        copies = len(NEAR) if d in DIRECT else 2
        arrive(("l", route, d), (first, count), {"z": at_z(d), middle: full(middle), last: (0, copies)})
        if d in DIRECT:
            whole_plane(route, d)
            return
        for way, m in enumerate(NEAR[:2]):
            sel = {"z": at_z(d), middle: half(middle, way), last: (shifted(pos, last, -m), 1)}
            push(("p", route, d), last, m, (first, count), sel)

    def from_last(route, d):
        first, count, middle, last = ROUTES[route]
        if d in DIRECT:
            return
        arrive(("p", route, d), (first, count), {"z": at_z(d), middle: full(middle)})
        whole_plane(route, d)

    def ring_sel(part, step, way, arriving):
        toward = 1 - 2 * way
        back = step if arriving else step - 1
        sel = {"z": (shifted(pos, "z", -toward * back), 1), "y": half("y", part), "x": full("x")}
        if step == SIZES["z"] // 2:
            sel["x"] = half("x", way)
        return sel

    def a_ring(step):
        steps = SIZES["z"] // 2
        for part in (0, 1):
            for way in (0, 1):
                if step > 1:
                    arrive(("r", part, step - 1, way), ROUTE_A, ring_sel(part, step - 1, way, True))
                if step <= steps:
                    push(("r", part, step, way), "z", 1 - 2 * way, ROUTE_A, ring_sel(part, step, way, False))
        for d in {1: (0,), steps + 1: (steps,)}.get(step, (step - 1, 1 - step)):
            hand_over(ROUTE_A, z=at_z(d), y=full("y"), x=full("x"))

    both = range(len(ROUTES))

    def begin(src):
        for route in both:
            for d in GROUPS[1]:
                to_z(route, d, src)
        for route in both:
            to_middle(route, 0, src)
        for m in NEAR:
            push(("y",), "y", m, ROUTE_A, {}, src)

    for which, ref in ((0, k_ref), (1, v_ref)):
        @pl.when(core == which)
        def _(ref=ref):
            sent_rows.clear()
            begin(ref)
    pltpu.make_async_copy(k_ref, all_ref.at[(core, *here)], own_sem).wait()
    blank[...] = jnp.zeros_like(blank)
    piece = blank.shape[0]
    pieces = zeros_ref.shape[0] // piece

    def wipe(at):
        return pltpu.make_async_copy(blank, zeros_ref.at[pl.ds(at * piece, piece)], zero_sem.at[at])

    for at in range(len(GROUPS) + 2):
        if at + 1 < len(GROUPS):
            for route in both:
                for d in GROUPS[at + 1]:
                    from_z(route, d)
                    to_middle(route, d)
        if at < len(GROUPS):
            for route in both:
                for d in GROUPS[at]:
                    from_middle(route, d)
                    to_last(route, d)
        if at == 0:
            arrive(("y",), ROUTE_A, {"y": (0, len(NEAR))})
            for m in NEAR:
                push(("x",), "x", m, ROUTE_A, {"y": full("y")})
        if at == 1:
            arrive(("x",), ROUTE_A, {"y": full("y"), "x": (0, len(NEAR))})
        if 0 < at <= SIZES["z"] // 2 + 1:
            a_ring(at)
        if 0 < at <= len(GROUPS):
            for route in both:
                for d in GROUPS[at - 1]:
                    pass_last(route, d)
        if 1 < at:
            for route in both:
                for d in GROUPS[at - 2]:
                    from_last(route, d)
        for i in range(at * 2, min(at * 2 + 2, pieces)):
            wipe(i).start()
    for at in range(pieces):
        wipe(at).wait()
    sent = zeros_ref.at[pl.ds(0, sum(sent_rows))]
    pltpu.make_async_remote_copy(
        src_ref=sent, dst_ref=sent, send_sem=send_sem, recv_sem=side_recv,
        device_id=(me, 1 - core), device_id_type=MESH,
    ).wait_send()
    side(all_ref.at[core]).wait_send()
    side(all_ref.at[1 - core]).wait_recv()


def gather_all(keys, values):
    dims = tuple(SIZES[axis] for axis in AXES)
    sems = pltpu.SemaphoreType.DMA((COPIES,))
    one_sem = pltpu.SemaphoreType.DMA
    piece = 2 * math.prod(dims) * ROWS // ZERO_PIECES
    anywhere = pl.BlockSpec(memory_space=pl.ANY)
    return pl.pallas_call(
        gather_kernel,
        out_shape=(
            jax.ShapeDtypeStruct((2, *dims, ROWS, HD), jnp.bfloat16),
            jax.ShapeDtypeStruct((ZERO_PIECES * piece, HD), jnp.bfloat16),
        ),
        in_specs=[anywhere, anywhere],
        out_specs=(anywhere, anywhere),
        scratch_shapes=[sems, one_sem, one_sem, one_sem, one_sem,
                        pltpu.SemaphoreType.DMA((ZERO_PIECES,)), pltpu.VMEM((piece, HD), jnp.bfloat16)],
        compiler_params=pltpu.CompilerParams(
            collective_id=0, has_side_effects=True, vmem_limit_bytes=VMEM_BYTES
        ),
    )(keys.reshape(1, 1, 1, ROWS, HD), values.reshape(1, 1, 1, ROWS, HD))


def reduce_kernel(
    terms_ref, dk_ref, dv_ref, held, other, final, ring_land, ax_land, ay_land, first_land, second_land,
    direct_land, middle_land, z_land, send, recv, load_sem, side_send, side_recv, last_send, last_recv,
):
    pos, me, core = my_place()
    sibling = (me, 1 - core)

    def load(d):
        z = shifted(pos, "z", d)
        return pltpu.make_async_copy(terms_ref.at[core, z], held.at[z], load_sem.at[d % 8])

    def side(d):
        z = shifted(pos, "z", d)
        return pltpu.make_async_remote_copy(
            src_ref=terms_ref.at[1 - core, z], dst_ref=other.at[z],
            send_sem=side_send, recv_sem=side_recv.at[d % 8],
            device_id=sibling, device_id_type=MESH,
        )

    far_first = GROUPS[::-1]
    for group in far_first:
        for d in group:
            load(d).start()
    greet(pos, me, core, Z_AWAY)
    for group in far_first:
        for d in group:
            side(d).start()

    number, kind = Numbers(), Numbers()

    def copy(key, axis, step, src, dst):
        return pltpu.make_async_remote_copy(
            src_ref=src, dst_ref=dst, send_sem=send.at[kind[key[0]]], recv_sem=recv.at[number[key]],
            device_id=peer(pos, core, axis, step), device_id_type=MESH,
        )

    def push(*item):
        copy(*item).start()

    def arrived(key, land):
        copy(key, "z", 1, land, land).wait_recv()

    def left(name, land):
        copy((name,), "z", 1, land, land).wait_send()

    def held_at(rows, **sel):
        index = []
        for axis in AXES:
            at = sel[axis] if axis in sel else pos[axis]
            index.append(pl.ds(*at) if isinstance(at, tuple) else at)
        return (*index, pl.ds(*rows), slice(None))

    def add(where, lands):
        total = as_f32(held[where])
        for land in lands:
            total = total + as_f32(land[...])
        held[where] = total.astype(jnp.bfloat16)

    def join(d):
        load(d).wait()
        side(d).wait_recv()
        z = shifted(pos, "z", d)

        def one(y, carry):
            for x in range(SIZES["x"]):
                held[z, y, x] = (as_f32(held[z, y, x]) + as_f32(other[z, y, x])).astype(jnp.bfloat16)
            return carry

        lax.fori_loop(0, SIZES["y"], one, 0)

    def middle_half(middle, way):
        size = SIZES[middle] // 2
        return (way * size, size)

    def first_copy(route, d, way):
        first, count, middle, last = ROUTES[route]
        where = {"z": shifted(pos, "z", d), middle: middle_half(middle, way), last: shifted(pos, last, 2)}
        return (("f", route, d), last, 1 - 2 * way, held.at[held_at((first, count), **where)],
                first_land.at[route, d % 8, way])

    def second_copy(route, d, way):
        first, count, middle, last = ROUTES[route]
        where = {"z": shifted(pos, "z", d), middle: (0, SIZES[middle]), last: shifted(pos, last, 1 - 2 * way)}
        return (("s", route, d), last, 1 - 2 * way, held.at[held_at((first, count), **where)],
                second_land.at[route, d % 8, way])

    def middle_copy(route, d, m):
        first, count, middle, last = ROUTES[route]
        where = {"z": shifted(pos, "z", d), middle: shifted(pos, middle, m)}
        return (("m", route, d), middle, m, held.at[held_at((first, count), **where)],
                middle_land.at[route, d % 8, NEAR.index(m)])

    def z_copy(route, d):
        first, count, _, _ = ROUTES[route]
        return (("z", route), "z", d, held.at[held_at((first, count), z=shifted(pos, "z", d))],
                z_land.at[route, Z_AWAY.index(d)])

    def direct_copy(route, d, m):
        first, count, middle, last = ROUTES[route]
        where = {"z": shifted(pos, "z", d), middle: (0, SIZES[middle]), last: shifted(pos, last, m)}
        return (("d", route, d), last, m, held.at[held_at((first, count), **where)],
                direct_land.at[route, SUM_DIRECT.index(d), NEAR.index(m)])

    def send_first(route, d):
        if d in SUM_DIRECT:
            for m in NEAR:
                push(*direct_copy(route, d, m))
            return
        for way in (0, 1):
            push(*first_copy(route, d, way))

    def send_second(route, d):
        first, count, middle, last = ROUTES[route]
        arrived(("f", route, d), first_land.at[route, d % 8])
        for way in (0, 1):
            low, size = middle_half(middle, way)
            for i in range(size):
                where = {"z": shifted(pos, "z", d), middle: low + i, last: shifted(pos, last, 1 - 2 * way)}
                add(held_at((first, count), **where), [first_land.at[route, d % 8, way, i]])
            push(*second_copy(route, d, way))

    def send_middle(route, d):
        first, count, middle, last = ROUTES[route]
        if d in SUM_DIRECT:
            arrived(("d", route, d), direct_land.at[route, SUM_DIRECT.index(d)])
            lands = [direct_land.at[route, SUM_DIRECT.index(d), i] for i in range(len(NEAR))]
        else:
            arrived(("s", route, d), second_land.at[route, d % 8])
            lands = [second_land.at[route, d % 8, way] for way in (0, 1)]
        for i in range(SIZES[middle]):
            where = {"z": shifted(pos, "z", d), middle: i}
            add(held_at((first, count), **where), [land.at[i] for land in lands])
        for m in NEAR:
            push(*middle_copy(route, d, m))

    def send_z(route, d):
        first, count, _, _ = ROUTES[route]
        arrived(("m", route, d), middle_land.at[route, d % 8])
        where = held_at((first, count), z=shifted(pos, "z", d))
        add(where, [middle_land.at[route, d % 8, i] for i in range(len(NEAR))])
        if d != 0:
            push(*z_copy(route, d))

    def ring_copy(step, way):
        toward = 1 - 2 * way
        half = SIZES["x"] // 2
        xs = (way * half, half) if step == 1 else (0, SIZES["x"])
        where = {"z": shifted(pos, "z", toward * (5 - step)), "y": (0, SIZES["y"]), "x": xs}
        return (("h" if step == 1 else "r", step, way), "z", toward, held.at[held_at(ROUTE_A, **where)],
                ring_land.at[way, step - 1, :, pl.ds(*xs)])

    def ring(step):
        for way in (0, 1):
            toward = 1 - 2 * way
            half = SIZES["x"] // 2
            if 1 < step < 5:
                copy(*ring_copy(step - 1, way)).wait_recv()
                low, size = (way * half, half) if step == 2 else (0, SIZES["x"])
                z = shifted(pos, "z", toward * (5 - step))

                def one(y, carry):
                    for i in range(size):
                        add(held_at(ROUTE_A, z=z, y=y, x=low + i), [ring_land.at[way, step - 2, y, low + i]])
                    return carry

                lax.fori_loop(0, SIZES["y"], one, 0)
            if step < 5:
                push(*ring_copy(step, way))
        if step == 5:
            for way in (0, 1):
                copy(*ring_copy(4, way)).wait_recv()

            def last(y, carry):
                for x in range(SIZES["x"]):
                    add(held_at(ROUTE_A, y=y, x=x), [ring_land.at[way, 3, y, x] for way in (0, 1)])
                return carry

            lax.fori_loop(0, SIZES["y"], last, 0)

    def ax_copy(m):
        where = {"y": (0, SIZES["y"]), "x": shifted(pos, "x", m)}
        return (("ax",), "x", m, held.at[held_at(ROUTE_A, **where)], ax_land.at[NEAR.index(m)])

    def ay_copy(m):
        where = {"y": shifted(pos, "y", m)}
        return (("ay",), "y", m, held.at[held_at(ROUTE_A, **where)], ay_land.at[NEAR.index(m)])

    both = range(len(ROUTES))
    for at in range(len(far_first) + 2):
        if at < len(far_first):
            for d in far_first[at]:
                join(d)
            for route in both:
                for d in far_first[at]:
                    send_first(route, d)
            ring(at + 1)
        if at == len(far_first) - 1:
            for m in NEAR:
                push(*ax_copy(m))
        for behind, act in ((1, send_second), (2, send_middle), (3, send_z)):
            for begun, group in enumerate(far_first):
                for d in group:
                    sooner = 1 if d in SUM_DIRECT else 0
                    if begun + behind - sooner == at and not (sooner and act is send_second):
                        for route in both:
                            act(route, d)
        if at == len(far_first):
            arrived(("ax",), ax_land)
            for y in range(SIZES["y"]):
                add(held_at(ROUTE_A, y=y), [ax_land.at[i, y] for i in range(len(NEAR))])
            for m in NEAR:
                push(*ay_copy(m))
    arrived(("ay",), ay_land)
    add(held_at(ROUTE_A), [ay_land.at[i] for i in range(len(NEAR))])
    for route in both:
        first, count, _, _ = ROUTES[route]
        arrived(("z", route), z_land.at[route])
        add(held_at((first, count)), [z_land.at[route, i] for i in range(len(Z_AWAY))])

    final[core] = held[pos["z"], pos["y"], pos["x"]]
    last_copy = pltpu.make_async_remote_copy(
        src_ref=final.at[core], dst_ref=final.at[core], send_sem=last_send, recv_sem=last_recv,
        device_id=sibling, device_id_type=MESH,
    )
    last_copy.start()
    pltpu.make_async_remote_copy(
        src_ref=other, dst_ref=other, send_sem=side_send, recv_sem=last_recv,
        device_id=sibling, device_id_type=MESH,
    ).wait_send()
    relayed = pl.ds(0, SIZES["z"] - len(SUM_DIRECT))
    left("f", first_land.at[:, relayed])
    left("s", second_land.at[:, relayed])
    left("d", direct_land)
    left("m", middle_land)
    left("z", z_land)
    left("h", ring_land.at[:, 0, :, pl.ds(0, SIZES["x"] // 2)])
    left("r", ring_land.at[:, pl.ds(1, 3)])
    left("ax", ax_land)
    left("ay", ay_land)
    last_copy.wait()
    dk_ref[...] = final[0]
    dv_ref[...] = final[1]


def reduce_all(terms):
    dims = tuple(SIZES[axis] for axis in AXES)
    nz, ny, nx = dims

    def vmem(*shape):
        return pltpu.VMEM((*shape, HD), jnp.bfloat16)

    count = ROUTES[0][1]
    routes = len(ROUTES)
    sems = pltpu.SemaphoreType.DMA((COPIES,))
    by_z = pltpu.SemaphoreType.DMA((nz,))
    one_sem = pltpu.SemaphoreType.DMA
    return pl.pallas_call(
        reduce_kernel,
        out_shape=(jax.ShapeDtypeStruct((ROWS, HD), jnp.bfloat16),) * 2,
        in_specs=[pl.BlockSpec(memory_space=pl.ANY)],
        out_specs=(pl.BlockSpec(memory_space=pltpu.VMEM),) * 2,
        scratch_shapes=[
            vmem(*dims, ROWS),
            vmem(*dims, ROWS),
            vmem(2, ROWS),
            vmem(2, nz // 2, ny, nx, ROUTE_A[1]),
            vmem(len(NEAR), ny, ROUTE_A[1]),
            vmem(len(NEAR), ROUTE_A[1]),
            vmem(routes, nz, 2, 2, count),
            vmem(routes, nz, 2, 4, count),
            vmem(routes, len(SUM_DIRECT), len(NEAR), 4, count),
            vmem(routes, nz, len(NEAR), count),
            vmem(routes, len(Z_AWAY), count),
            pltpu.SemaphoreType.DMA((9,)), sems, by_z, one_sem, by_z, one_sem, one_sem,
        ],
        compiler_params=pltpu.CompilerParams(
            collective_id=1, has_side_effects=True, vmem_limit_bytes=VMEM_BYTES
        ),
    )(terms)


def dot(left, right, contract):
    return lax.dot_general(
        left, right, ((contract[:1], contract[1:]), ((), ())), preferred_element_type=jnp.float32
    )


def over_blocks(count, step, carry):
    done = jnp.int32(0)
    for size in STEPS:
        steps = (count - done) // size
        carry = lax.fori_loop(
            0, steps, lambda at, c, done=done, size=size: step(done + at * size, size, c), carry
        )
        done = done + steps * size
    return carry


def attention_kernel(
    starts_ref, assign_ref, q_ref, g_ref, kv_ref, zeros_ref, out_ref, dq_ref, terms_ref,
    place_ref, tiles, sums, scores, probs, q_cols, g_cols, acc, in_sem, out_sem,
):
    del zeros_ref
    heads = q_ref.shape[1] // HD
    cols = heads * SPAN
    scale = 1.0 / math.sqrt(HD)
    to_exp2 = scale * math.log2(math.e)
    per_block = BLOCK // SPAN

    def locate(at, carry):
        for i in range(16):
            place_ref[assign_ref[at * 16 + i]] = at * 16 + i
        return carry

    lax.fori_loop(0, assign_ref.shape[0] // 16, locate, 0)
    first_span = lax.axis_index("ctx") * 2
    bases, firsts, lasts = [], [], []
    for part in range(2):
        base = assign_ref[first_span + part] * SPAN
        doc_first = jnp.int32(0)
        for doc in range(starts_ref.shape[0]):
            start = starts_ref[doc]
            doc_first = jnp.where(start <= base, jnp.maximum(doc_first, start), doc_first)
        bases.append(base)
        firsts.append(doc_first // BLOCK)
        lasts.append(base // BLOCK)

    def rows_at(at, count):
        return pl.ds(pl.multiple_of(at * count, count), count)

    def stored(block, i):
        return rows_at(place_ref[block * per_block + i], SPAN)

    def fetch(part, at):
        for i in range(per_block):
            pltpu.make_async_copy(
                kv_ref.at[:, stored(firsts[part] + at, i), :],
                tiles.at[part, :, rows_at(at * per_block + i, SPAN), :],
                in_sem.at[part, at],
            ).start()

    def fetched(part, at):
        pltpu.make_async_copy(
            kv_ref.at[:, pl.ds(0, BLOCK), :], tiles.at[part, :, rows_at(at, BLOCK), :], in_sem.at[part, at]
        ).wait()

    def store(block):
        for i in range(per_block):
            pltpu.make_async_copy(
                sums.at[:, rows_at(block * per_block + i, SPAN), :],
                terms_ref.at[:, stored(block, i), :],
                out_sem.at[block],
            ).start()

    def stored_all(block):
        pltpu.make_async_copy(
            sums.at[:, rows_at(block, BLOCK), :], terms_ref.at[:, pl.ds(0, BLOCK), :], out_sem.at[block]
        ).wait()

    def shared(block):
        return (block >= firsts[1]) & (block <= lasts[1])

    for part in range(2):
        lax.fori_loop(0, lasts[part] - firsts[part] + 1, lambda at, c, part=part: (fetch(part, at), c)[1], 0)

    for part in range(2):
        base = bases[part]
        full_blocks = lasts[part] - firsts[part]
        inside = base - lasts[part] * BLOCK

        rows = pl.ds(part * SPAN, SPAN)
        q_rows = jnp.concatenate(
            [q_ref[rows, h * HD : (h + 1) * HD] for h in range(heads)], axis=0
        )
        g_rows = jnp.concatenate(
            [g_ref[rows, h * HD : (h + 1) * HD] for h in range(heads)], axis=0
        )
        q_t = as_f32(q_rows).T
        g_t = as_f32(g_rows).T
        q_cols[...] = q_t.astype(jnp.bfloat16)
        g_cols[...] = g_t.astype(jnp.bfloat16)

        def keys_at(at, size):
            return pl.ds(pl.multiple_of(at * BLOCK, BLOCK), size * BLOCK)

        def tile(which, at, size, part=part):
            return tiles[part, which, keys_at(at, size), :]

        def fold(value, op):
            value = value.reshape(value.shape[0] // 8, 8, cols)
            return op(value, axis=0)

        def score_step(at, size, top, part=part):
            for i in range(size):
                fetched(part, at + i)
            s = dot(tile(0, at, size), q_cols[...], (1, 0))
            scores[keys_at(at, size), :] = s
            return jnp.maximum(top, fold(s, jnp.max))

        top = over_blocks(full_blocks, score_step, jnp.full((8, cols), -1e30, jnp.float32))
        fetched(part, full_blocks)
        s = dot(tile(0, full_blocks, 1), q_cols[...], (1, 0))
        key_at = lax.broadcasted_iota(jnp.int32, (BLOCK, cols), 0)
        query_at = lax.broadcasted_iota(jnp.int32, (BLOCK, cols), 1)
        s = jnp.where(key_at <= inside + lax.rem(query_at, SPAN), s, -1e30)
        scores[keys_at(full_blocks, 1), :] = s
        top = jnp.max(jnp.maximum(top, fold(s, jnp.max)), axis=0, keepdims=True)

        acc[...] = jnp.zeros_like(acc)

        def value_step(at, size, total):
            p = jnp.exp2((scores[keys_at(at, size), :] - top) * to_exp2)
            p16 = p.astype(jnp.bfloat16)
            probs[keys_at(at, size), :] = p16
            acc[...] += dot(tile(1, at, size), p16, (0, 0))
            return total + fold(p, jnp.sum)

        total = over_blocks(full_blocks + 1, value_step, jnp.zeros((8, cols), jnp.float32))
        inverse = 1.0 / jnp.sum(total, axis=0, keepdims=True)
        out_t = (acc[...] * inverse).astype(jnp.bfloat16).astype(jnp.float32)
        delta = jnp.sum(g_t * out_t, axis=0, keepdims=True)
        q_scaled = (q_t * (inverse * scale)).astype(jnp.bfloat16)
        g_scaled = (g_t * inverse).astype(jnp.bfloat16)
        out_rows = out_t.T.astype(jnp.bfloat16)
        acc[...] = jnp.zeros_like(acc)

        def grad_step(at, size, carry, part=part):
            p16 = probs[keys_at(at, size), :]
            keys = tile(0, at, size)
            d_probs = dot(tile(1, at, size), g_cols[...], (1, 0))
            d_scores = (as_f32(p16) * (d_probs - delta)).astype(jnp.bfloat16)
            acc[...] += dot(keys, d_scores, (0, 0))
            d_key = dot(d_scores, q_scaled, (1, 1))
            d_value = dot(p16, g_scaled, (1, 1))
            for i in range(size):
                block = firsts[part] + at + i
                here = rows_at(block, BLOCK)
                for which, term in ((0, d_key), (1, d_value)):
                    term = term[i * BLOCK : (i + 1) * BLOCK]
                    if part > 0:
                        both = (block >= firsts[0]) & (block <= lasts[0])
                        term = term + jnp.where(both, as_f32(sums[which, here, :]), 0.0)
                    sums[which, here, :] = term.astype(jnp.bfloat16)
                if part > 0:
                    store(block)
                else:
                    pl.when(jnp.logical_not(shared(block)))(lambda block=block: store(block))
            return carry

        over_blocks(full_blocks + 1, grad_step, 0)
        dq_rows = (acc[...] * (inverse * scale)).T.astype(jnp.bfloat16)
        for h in range(heads):
            out_ref[rows, h * HD : (h + 1) * HD] = out_rows[h * SPAN : (h + 1) * SPAN]
            dq_ref[rows, h * HD : (h + 1) * HD] = dq_rows[h * SPAN : (h + 1) * SPAN]

    def drain(block, carry, part):
        if part > 0:
            stored_all(block)
        else:
            pl.when(jnp.logical_not(shared(block)))(lambda: stored_all(block))
        return carry

    for part in range(2):
        lax.fori_loop(firsts[part], lasts[part] + 1, lambda block, c, part=part: drain(block, c, part), 0)


def attention(doc_starts, assign, queries, d_out, kv_all, zeros):
    tokens = kv_all.shape[1]
    heads = queries.shape[1] // HD
    cols = heads * SPAN
    longest = tokens - (doc_starts.shape[0] - 1) * UNIT
    blocks = -(-longest // BLOCK)
    smem = pl.BlockSpec(memory_space=pltpu.SMEM)
    vmem = pl.BlockSpec(memory_space=pltpu.VMEM)
    anywhere = pl.BlockSpec(memory_space=pl.ANY)
    return pl.pallas_call(
        attention_kernel,
        out_shape=(
            jax.ShapeDtypeStruct(queries.shape, jnp.bfloat16),
            jax.ShapeDtypeStruct(queries.shape, jnp.bfloat16),
            jax.ShapeDtypeStruct(zeros.shape, jnp.bfloat16),
        ),
        in_specs=[smem, smem, vmem, vmem, anywhere, anywhere],
        out_specs=(vmem, vmem, anywhere),
        input_output_aliases={5: 2},
        scratch_shapes=[
            pltpu.SMEM(assign.shape, jnp.int32),
            pltpu.VMEM((2, 2, blocks * BLOCK, HD), jnp.bfloat16),
            pltpu.VMEM((2, tokens, HD), jnp.bfloat16),
            pltpu.VMEM((blocks * BLOCK, cols), jnp.float32),
            pltpu.VMEM((blocks * BLOCK, cols), jnp.bfloat16),
            pltpu.VMEM((HD, cols), jnp.bfloat16),
            pltpu.VMEM((HD, cols), jnp.bfloat16),
            pltpu.VMEM((HD, cols), jnp.float32),
            pltpu.SemaphoreType.DMA((2, blocks)),
            pltpu.SemaphoreType.DMA((tokens // BLOCK,)),
        ],
        compiler_params=pltpu.CompilerParams(vmem_limit_bytes=VMEM_BYTES),
    )(doc_starts, assign, queries, d_out, kv_all, zeros)


def body(queries, keys, values, d_out, doc_starts, assign):
    tokens = assign.shape[0] * SPAN
    dims = tuple(SIZES[axis] for axis in AXES)
    kv_all, zeros = gather_all(keys, values)
    attn_out, d_query, terms = attention(
        doc_starts, assign, queries, d_out, kv_all.reshape(2, tokens, HD), zeros.reshape(2, tokens, HD)
    )
    d_key, d_value = reduce_all(terms.reshape(2, *dims, ROWS, HD))
    return (attn_out, d_query, d_key, d_value)


def solution(mesh):
    placed = (P("ctx", "head"), P("ctx", None), P("ctx", None), P("ctx", "head"), P(), P())
    return jax.shard_map(
        body,
        mesh=mesh,
        in_specs=placed,
        out_specs=(P("ctx", "head"), P("ctx", "head"), P("ctx", None), P("ctx", None)),
        check_vma=False,
    )
```

```python
import math

import jax
import jax.numpy as jnp
from jax import lax
from jax.experimental import pallas as pl
from jax.experimental.pallas import tpu as pltpu
from jax.sharding import PartitionSpec as P

HD = 128
SPAN = 64
ROWS = 2 * SPAN
BLOCK = 512
UNIT = 512
STEPS = (4, 2, 1)
MESH = pl.DeviceIdType.MESH
AXES = ("z", "y", "x")
SIZES = {"z": 8, "y": 4, "x": 4}
ROUTE_A = (0, 32)
ROUTES = ((32, 48, "y", "x"), (80, 48, "x", "y"))
NEAR = (1, -1, 2)
Z_AWAY = (1, -1, 2, -2, 3, -3, 4)
GROUPS = ((0,), (1, -1), (2, -2), (3, -3), (4,))
DIRECT = (4, 3, -3)
SUM_DIRECT = (0, 1, -1)
COPIES = 74
ZERO_PIECES = 8
VMEM_BYTES = 60 * 1024 * 1024


def my_place():
    me = lax.axis_index("ctx")
    nx, ny = SIZES["x"], SIZES["y"]
    pos = {"x": lax.rem(me, nx), "y": lax.rem(me // nx, ny), "z": me // (nx * ny)}
    return pos, me, lax.axis_index("head")


def wrapped(value, size):
    return lax.rem(value + 2 * size, size)


def shifted(pos, axis, step):
    return wrapped(pos[axis] + step, SIZES[axis])


def peer(pos, core, axis, step):
    there = dict(pos)
    there[axis] = shifted(pos, axis, step)
    return ((there["z"] * SIZES["y"] + there["y"]) * SIZES["x"] + there["x"], core)


def greet(pos, me, core, along_z):
    barrier = pltpu.get_barrier_semaphore()
    partners = [("z", step) for step in along_z] + [(axis, step) for axis in "yx" for step in NEAR]
    for axis, step in partners:
        pl.semaphore_signal(
            barrier, inc=1, device_id=peer(pos, core, axis, step), device_id_type=MESH
        )
    pl.semaphore_signal(barrier, inc=1, device_id=(me, 1 - core), device_id_type=MESH)
    pl.semaphore_wait(barrier, len(partners) + 1)


def as_f32(value):
    return value.astype(jnp.float32)


class Numbers(dict):
    def __missing__(self, key):
        self[key] = len(self)
        assert len(self) <= COPIES
        return self[key]


def gather_kernel(
    k_ref, v_ref, all_ref, zeros_ref, recv, send_sem, side_send, side_recv, own_sem, zero_sem, blank
):
    pos, me, core = my_place()
    here = tuple(pl.ds(pos[axis], 1) for axis in AXES)
    for which, ref in ((0, k_ref), (1, v_ref)):
        @pl.when(core == which)
        def _(ref=ref):
            pltpu.make_async_copy(ref, all_ref.at[(core, *here)], own_sem).start()
    greet(pos, me, core, (1, -1))

    number = Numbers()
    sent_rows = []

    def view(owner, rows, **sel):
        index = [sel[axis] if axis in sel else (pos[axis], 1) for axis in AXES]
        return all_ref.at[(owner, *(pl.ds(*at) for at in index), pl.ds(*rows), slice(None))]

    def push(key, axis, step, rows, sel, src=None):
        ref = view(core, rows, **sel)
        pltpu.make_async_remote_copy(
            src_ref=ref if src is None else src.at[:, :, :, pl.ds(*rows), :],
            dst_ref=ref, send_sem=send_sem, recv_sem=recv.at[number[key]],
            device_id=peer(pos, core, axis, step), device_id_type=MESH,
        ).start()
        sent_rows.append(rows[1] * math.prod(count for _, count in sel.values()))

    def arrive(key, rows, sel):
        ref = view(core, rows, **sel)
        pltpu.make_async_remote_copy(
            src_ref=ref, dst_ref=ref, send_sem=send_sem, recv_sem=recv.at[number[key]],
            device_id=(me, 1 - core), device_id_type=MESH,
        ).wait_recv()

    def side(ref):
        return pltpu.make_async_remote_copy(
            src_ref=ref, dst_ref=ref, send_sem=side_send, recv_sem=side_recv,
            device_id=(me, 1 - core), device_id_type=MESH,
        )

    def hand_over(rows, **sel):
        side(view(core, rows, **sel)).start()

    def full(axis):
        return (0, SIZES[axis])

    def half(axis, side_at):
        return (side_at * (SIZES[axis] // 2), SIZES[axis] // 2)

    def z_way(route, d):
        if d == 4:
            return 1 - 2 * route
        return -1 if d > 0 else 1

    def at_z(d):
        return (shifted(pos, "z", d), 1)

    def to_z(route, d, src=None):
        first, count, _, _ = ROUTES[route]
        toward = z_way(route, d)
        push(("z", route, d), "z", toward, (first, count), {"z": at_z(d + toward)}, src)

    def from_z(route, d):
        first, count, _, _ = ROUTES[route]
        arrive(("z", route, d), (first, count), {"z": at_z(d)})
        if abs(d) < 3:
            to_z(route, d - z_way(route, d))
        elif d != 4 and z_way(route, d) == z_way(route, 4):
            to_z(route, 4)

    def to_middle(route, d, src=None):
        first, count, middle, _ = ROUTES[route]
        for m in NEAR:
            push(("m", route, d), middle, m, (first, count), {"z": at_z(d)}, src)

    def from_middle(route, d):
        first, count, middle, _ = ROUTES[route]
        arrive(("m", route, d), (first, count), {"z": at_z(d), middle: (0, len(NEAR))})

    def to_last(route, d):
        first, count, middle, last = ROUTES[route]
        sel = {"z": at_z(d), middle: full(middle)}
        for m in (NEAR if d in DIRECT else NEAR[:2]):
            push(("l", route, d), last, m, (first, count), sel)

    def whole_plane(route, d):
        first, count, _, _ = ROUTES[route]
        hand_over((first, count), z=at_z(d), y=full("y"), x=full("x"))

    def pass_last(route, d):
        first, count, middle, last = ROUTES[route]
        copies = len(NEAR) if d in DIRECT else 2
        arrive(("l", route, d), (first, count), {"z": at_z(d), middle: full(middle), last: (0, copies)})
        if d in DIRECT:
            whole_plane(route, d)
            return
        for way, m in enumerate(NEAR[:2]):
            sel = {"z": at_z(d), middle: half(middle, way), last: (shifted(pos, last, -m), 1)}
            push(("p", route, d), last, m, (first, count), sel)

    def from_last(route, d):
        first, count, middle, last = ROUTES[route]
        if d in DIRECT:
            return
        arrive(("p", route, d), (first, count), {"z": at_z(d), middle: full(middle)})
        whole_plane(route, d)

    def ring_sel(part, step, way, arriving):
        toward = 1 - 2 * way
        back = step if arriving else step - 1
        sel = {"z": (shifted(pos, "z", -toward * back), 1), "y": half("y", part), "x": full("x")}
        if step == SIZES["z"] // 2:
            sel["x"] = half("x", way)
        return sel

    def a_ring(step):
        steps = SIZES["z"] // 2
        for part in (0, 1):
            for way in (0, 1):
                if step > 1:
                    arrive(("r", part, step - 1, way), ROUTE_A, ring_sel(part, step - 1, way, True))
                if step <= steps:
                    push(("r", part, step, way), "z", 1 - 2 * way, ROUTE_A, ring_sel(part, step, way, False))
        for d in {1: (0,), steps + 1: (steps,)}.get(step, (step - 1, 1 - step)):
            hand_over(ROUTE_A, z=at_z(d), y=full("y"), x=full("x"))

    both = range(len(ROUTES))

    def begin(src):
        for route in both:
            for d in GROUPS[1]:
                to_z(route, d, src)
        for route in both:
            to_middle(route, 0, src)
        for m in NEAR:
            push(("y",), "y", m, ROUTE_A, {}, src)

    for which, ref in ((0, k_ref), (1, v_ref)):
        @pl.when(core == which)
        def _(ref=ref):
            sent_rows.clear()
            begin(ref)
    pltpu.make_async_copy(k_ref, all_ref.at[(core, *here)], own_sem).wait()
    blank[...] = jnp.zeros_like(blank)
    piece = blank.shape[0]
    pieces = zeros_ref.shape[0] // piece

    def wipe(at):
        return pltpu.make_async_copy(blank, zeros_ref.at[pl.ds(at * piece, piece)], zero_sem.at[at])

    for at in range(len(GROUPS) + 2):
        if at + 1 < len(GROUPS):
            for route in both:
                for d in GROUPS[at + 1]:
                    from_z(route, d)
                    to_middle(route, d)
        if at < len(GROUPS):
            for route in both:
                for d in GROUPS[at]:
                    from_middle(route, d)
                    to_last(route, d)
        if at == 0:
            arrive(("y",), ROUTE_A, {"y": (0, len(NEAR))})
            for m in NEAR:
                push(("x",), "x", m, ROUTE_A, {"y": full("y")})
        if at == 1:
            arrive(("x",), ROUTE_A, {"y": full("y"), "x": (0, len(NEAR))})
        if 0 < at <= SIZES["z"] // 2 + 1:
            a_ring(at)
        if 0 < at <= len(GROUPS):
            for route in both:
                for d in GROUPS[at - 1]:
                    pass_last(route, d)
        if 1 < at:
            for route in both:
                for d in GROUPS[at - 2]:
                    from_last(route, d)
        for i in range(at * 2, min(at * 2 + 2, pieces)):
            wipe(i).start()
    for at in range(pieces):
        wipe(at).wait()
    sent = zeros_ref.at[pl.ds(0, sum(sent_rows))]
    pltpu.make_async_remote_copy(
        src_ref=sent, dst_ref=sent, send_sem=send_sem, recv_sem=side_recv,
        device_id=(me, 1 - core), device_id_type=MESH,
    ).wait_send()
    side(all_ref.at[core]).wait_send()
    side(all_ref.at[1 - core]).wait_recv()


def gather_all(keys, values):
    dims = tuple(SIZES[axis] for axis in AXES)
    sems = pltpu.SemaphoreType.DMA((COPIES,))
    one_sem = pltpu.SemaphoreType.DMA
    piece = 2 * math.prod(dims) * ROWS // ZERO_PIECES
    anywhere = pl.BlockSpec(memory_space=pl.ANY)
    return pl.pallas_call(
        gather_kernel,
        out_shape=(
            jax.ShapeDtypeStruct((2, *dims, ROWS, HD), jnp.bfloat16),
            jax.ShapeDtypeStruct((ZERO_PIECES * piece, HD), jnp.bfloat16),
        ),
        in_specs=[anywhere, anywhere],
        out_specs=(anywhere, anywhere),
        scratch_shapes=[sems, one_sem, one_sem, one_sem, one_sem,
                        pltpu.SemaphoreType.DMA((ZERO_PIECES,)), pltpu.VMEM((piece, HD), jnp.bfloat16)],
        compiler_params=pltpu.CompilerParams(
            collective_id=0, has_side_effects=True, vmem_limit_bytes=VMEM_BYTES
        ),
    )(keys.reshape(1, 1, 1, ROWS, HD), values.reshape(1, 1, 1, ROWS, HD))


def reduce_kernel(
    terms_ref, out_ref, held, other, final, ring_land, ax_land, ay_land, first_land, second_land,
    direct_land, middle_land, z_land, send, recv, load_sem, side_send, side_recv, last_send, last_recv,
):
    pos, me, core = my_place()
    sibling = (me, 1 - core)

    def load(d):
        z = shifted(pos, "z", d)
        return pltpu.make_async_copy(terms_ref.at[core, z], held.at[z], load_sem.at[d % 8])

    def side(d):
        z = shifted(pos, "z", d)
        return pltpu.make_async_remote_copy(
            src_ref=terms_ref.at[1 - core, z], dst_ref=other.at[z],
            send_sem=side_send, recv_sem=side_recv.at[d % 8],
            device_id=sibling, device_id_type=MESH,
        )

    far_first = GROUPS[::-1]
    for group in far_first:
        for d in group:
            load(d).start()
    greet(pos, me, core, Z_AWAY)
    for group in far_first:
        for d in group:
            side(d).start()

    number, kind = Numbers(), Numbers()

    def copy(key, axis, step, src, dst):
        return pltpu.make_async_remote_copy(
            src_ref=src, dst_ref=dst, send_sem=send.at[kind[key[0]]], recv_sem=recv.at[number[key]],
            device_id=peer(pos, core, axis, step), device_id_type=MESH,
        )

    def push(*item):
        copy(*item).start()

    def arrived(key, land):
        copy(key, "z", 1, land, land).wait_recv()

    def left(name, land):
        copy((name,), "z", 1, land, land).wait_send()

    def held_at(rows, **sel):
        index = []
        for axis in AXES:
            at = sel[axis] if axis in sel else pos[axis]
            index.append(pl.ds(*at) if isinstance(at, tuple) else at)
        return (*index, pl.ds(*rows), slice(None))

    def add(where, lands):
        total = as_f32(held[where])
        for land in lands:
            total = total + as_f32(land[...])
        held[where] = total.astype(jnp.bfloat16)

    def join(d):
        load(d).wait()
        side(d).wait_recv()
        z = shifted(pos, "z", d)

        def one(y, carry):
            for x in range(SIZES["x"]):
                held[z, y, x] = (as_f32(held[z, y, x]) + as_f32(other[z, y, x])).astype(jnp.bfloat16)
            return carry

        lax.fori_loop(0, SIZES["y"], one, 0)

    def middle_half(middle, way):
        size = SIZES[middle] // 2
        return (way * size, size)

    def first_copy(route, d, way):
        first, count, middle, last = ROUTES[route]
        where = {"z": shifted(pos, "z", d), middle: middle_half(middle, way), last: shifted(pos, last, 2)}
        return (("f", route, d), last, 1 - 2 * way, held.at[held_at((first, count), **where)],
                first_land.at[route, d % 8, way])

    def second_copy(route, d, way):
        first, count, middle, last = ROUTES[route]
        where = {"z": shifted(pos, "z", d), middle: (0, SIZES[middle]), last: shifted(pos, last, 1 - 2 * way)}
        return (("s", route, d), last, 1 - 2 * way, held.at[held_at((first, count), **where)],
                second_land.at[route, d % 8, way])

    def middle_copy(route, d, m):
        first, count, middle, last = ROUTES[route]
        where = {"z": shifted(pos, "z", d), middle: shifted(pos, middle, m)}
        return (("m", route, d), middle, m, held.at[held_at((first, count), **where)],
                middle_land.at[route, d % 8, NEAR.index(m)])

    def z_copy(route, d):
        first, count, _, _ = ROUTES[route]
        return (("z", route), "z", d, held.at[held_at((first, count), z=shifted(pos, "z", d))],
                z_land.at[route, Z_AWAY.index(d)])

    def direct_copy(route, d, m):
        first, count, middle, last = ROUTES[route]
        where = {"z": shifted(pos, "z", d), middle: (0, SIZES[middle]), last: shifted(pos, last, m)}
        return (("d", route, d), last, m, held.at[held_at((first, count), **where)],
                direct_land.at[route, SUM_DIRECT.index(d), NEAR.index(m)])

    def send_first(route, d):
        if d in SUM_DIRECT:
            for m in NEAR:
                push(*direct_copy(route, d, m))
            return
        for way in (0, 1):
            push(*first_copy(route, d, way))

    def send_second(route, d):
        first, count, middle, last = ROUTES[route]
        arrived(("f", route, d), first_land.at[route, d % 8])
        for way in (0, 1):
            low, size = middle_half(middle, way)
            for i in range(size):
                where = {"z": shifted(pos, "z", d), middle: low + i, last: shifted(pos, last, 1 - 2 * way)}
                add(held_at((first, count), **where), [first_land.at[route, d % 8, way, i]])
            push(*second_copy(route, d, way))

    def send_middle(route, d):
        first, count, middle, last = ROUTES[route]
        if d in SUM_DIRECT:
            arrived(("d", route, d), direct_land.at[route, SUM_DIRECT.index(d)])
            lands = [direct_land.at[route, SUM_DIRECT.index(d), i] for i in range(len(NEAR))]
        else:
            arrived(("s", route, d), second_land.at[route, d % 8])
            lands = [second_land.at[route, d % 8, way] for way in (0, 1)]
        for i in range(SIZES[middle]):
            where = {"z": shifted(pos, "z", d), middle: i}
            add(held_at((first, count), **where), [land.at[i] for land in lands])
        for m in NEAR:
            push(*middle_copy(route, d, m))

    def send_z(route, d):
        first, count, _, _ = ROUTES[route]
        arrived(("m", route, d), middle_land.at[route, d % 8])
        where = held_at((first, count), z=shifted(pos, "z", d))
        add(where, [middle_land.at[route, d % 8, i] for i in range(len(NEAR))])
        if d != 0:
            push(*z_copy(route, d))

    def ring_copy(step, way):
        toward = 1 - 2 * way
        half = SIZES["x"] // 2
        xs = (way * half, half) if step == 1 else (0, SIZES["x"])
        where = {"z": shifted(pos, "z", toward * (5 - step)), "y": (0, SIZES["y"]), "x": xs}
        return (("h" if step == 1 else "r", step, way), "z", toward, held.at[held_at(ROUTE_A, **where)],
                ring_land.at[way, step - 1, :, pl.ds(*xs)])

    def ring(step):
        for way in (0, 1):
            toward = 1 - 2 * way
            half = SIZES["x"] // 2
            if 1 < step < 5:
                copy(*ring_copy(step - 1, way)).wait_recv()
                low, size = (way * half, half) if step == 2 else (0, SIZES["x"])
                z = shifted(pos, "z", toward * (5 - step))

                def one(y, carry):
                    for i in range(size):
                        add(held_at(ROUTE_A, z=z, y=y, x=low + i), [ring_land.at[way, step - 2, y, low + i]])
                    return carry

                lax.fori_loop(0, SIZES["y"], one, 0)
            if step < 5:
                push(*ring_copy(step, way))
        if step == 5:
            for way in (0, 1):
                copy(*ring_copy(4, way)).wait_recv()

            def last(y, carry):
                for x in range(SIZES["x"]):
                    add(held_at(ROUTE_A, y=y, x=x), [ring_land.at[way, 3, y, x] for way in (0, 1)])
                return carry

            lax.fori_loop(0, SIZES["y"], last, 0)

    def ax_copy(m):
        where = {"y": (0, SIZES["y"]), "x": shifted(pos, "x", m)}
        return (("ax",), "x", m, held.at[held_at(ROUTE_A, **where)], ax_land.at[NEAR.index(m)])

    def ay_copy(m):
        where = {"y": shifted(pos, "y", m)}
        return (("ay",), "y", m, held.at[held_at(ROUTE_A, **where)], ay_land.at[NEAR.index(m)])

    both = range(len(ROUTES))
    for at in range(len(far_first) + 2):
        if at < len(far_first):
            for d in far_first[at]:
                join(d)
            for route in both:
                for d in far_first[at]:
                    send_first(route, d)
        for behind, act in ((1, send_second), (2, send_middle), (3, send_z)):
            for begun, group in enumerate(far_first):
                for d in group:
                    sooner = 1 if d in SUM_DIRECT else 0
                    if begun + behind - sooner == at and not (sooner and act is send_second):
                        for route in both:
                            act(route, d)
        if at < len(far_first):
            ring(at + 1)
        if at == len(far_first) - 1:
            for m in NEAR:
                push(*ax_copy(m))
        if at == len(far_first):
            arrived(("ax",), ax_land)
            for y in range(SIZES["y"]):
                add(held_at(ROUTE_A, y=y), [ax_land.at[i, y] for i in range(len(NEAR))])
            for m in NEAR:
                push(*ay_copy(m))
    arrived(("ay",), ay_land)
    add(held_at(ROUTE_A), [ay_land.at[i] for i in range(len(NEAR))])
    for route in both:
        first, count, _, _ = ROUTES[route]
        arrived(("z", route), z_land.at[route])
        add(held_at((first, count)), [z_land.at[route, i] for i in range(len(Z_AWAY))])

    final[core] = held[pos["z"], pos["y"], pos["x"]]
    last_copy = pltpu.make_async_remote_copy(
        src_ref=final.at[core], dst_ref=final.at[core], send_sem=last_send, recv_sem=last_recv,
        device_id=sibling, device_id_type=MESH,
    )
    last_copy.start()
    pltpu.make_async_remote_copy(
        src_ref=other, dst_ref=other, send_sem=side_send, recv_sem=last_recv,
        device_id=sibling, device_id_type=MESH,
    ).wait_send()
    relayed = pl.ds(0, SIZES["z"] - len(SUM_DIRECT))
    left("f", first_land.at[:, relayed])
    left("s", second_land.at[:, relayed])
    left("d", direct_land)
    left("m", middle_land)
    left("z", z_land)
    left("h", ring_land.at[:, 0, :, pl.ds(0, SIZES["x"] // 2)])
    left("r", ring_land.at[:, pl.ds(1, 3)])
    left("ax", ax_land)
    left("ay", ay_land)
    last_copy.wait()
    out_ref[...] = final[...]


def reduce_all(terms):
    dims = tuple(SIZES[axis] for axis in AXES)
    nz, ny, nx = dims

    def vmem(*shape):
        return pltpu.VMEM((*shape, HD), jnp.bfloat16)

    count = ROUTES[0][1]
    routes = len(ROUTES)
    sems = pltpu.SemaphoreType.DMA((COPIES,))
    by_z = pltpu.SemaphoreType.DMA((nz,))
    one_sem = pltpu.SemaphoreType.DMA
    return pl.pallas_call(
        reduce_kernel,
        out_shape=jax.ShapeDtypeStruct((2, ROWS, HD), jnp.bfloat16),
        in_specs=[pl.BlockSpec(memory_space=pl.ANY)],
        out_specs=pl.BlockSpec(memory_space=pltpu.VMEM),
        scratch_shapes=[
            vmem(*dims, ROWS),
            vmem(*dims, ROWS),
            vmem(2, ROWS),
            vmem(2, nz // 2, ny, nx, ROUTE_A[1]),
            vmem(len(NEAR), ny, ROUTE_A[1]),
            vmem(len(NEAR), ROUTE_A[1]),
            vmem(routes, nz, 2, 2, count),
            vmem(routes, nz, 2, 4, count),
            vmem(routes, len(SUM_DIRECT), len(NEAR), 4, count),
            vmem(routes, nz, len(NEAR), count),
            vmem(routes, len(Z_AWAY), count),
            pltpu.SemaphoreType.DMA((9,)), sems, by_z, one_sem, by_z, one_sem, one_sem,
        ],
        compiler_params=pltpu.CompilerParams(
            collective_id=1, has_side_effects=True, vmem_limit_bytes=VMEM_BYTES
        ),
    )(terms)


def dot(left, right, contract):
    return lax.dot_general(
        left, right, ((contract[:1], contract[1:]), ((), ())), preferred_element_type=jnp.float32
    )


def over_blocks(count, step, carry):
    done = jnp.int32(0)
    for size in STEPS:
        steps = (count - done) // size
        carry = lax.fori_loop(
            0, steps, lambda at, c, done=done, size=size: step(done + at * size, size, c), carry
        )
        done = done + steps * size
    return carry


def attention_kernel(
    starts_ref, assign_ref, q_ref, g_ref, kv_ref, zeros_ref, out_ref, dq_ref, terms_ref,
    place_ref, tiles, sums, scores, probs, q_cols, g_cols, acc, in_sem, out_sem,
):
    del zeros_ref
    heads = q_ref.shape[1] // HD
    cols = heads * SPAN
    scale = 1.0 / math.sqrt(HD)
    to_exp2 = scale * math.log2(math.e)
    per_block = BLOCK // SPAN

    def locate(at, carry):
        for i in range(16):
            place_ref[assign_ref[at * 16 + i]] = at * 16 + i
        return carry

    lax.fori_loop(0, assign_ref.shape[0] // 16, locate, 0)
    first_span = lax.axis_index("ctx") * 2
    bases, firsts, lasts = [], [], []
    for part in range(2):
        base = assign_ref[first_span + part] * SPAN
        doc_first = jnp.int32(0)
        for doc in range(starts_ref.shape[0]):
            start = starts_ref[doc]
            doc_first = jnp.where(start <= base, jnp.maximum(doc_first, start), doc_first)
        bases.append(base)
        firsts.append(doc_first // BLOCK)
        lasts.append(base // BLOCK)

    def rows_at(at, count):
        return pl.ds(pl.multiple_of(at * count, count), count)

    def stored(block, i):
        return rows_at(place_ref[block * per_block + i], SPAN)

    def fetch(part, at):
        for i in range(per_block):
            pltpu.make_async_copy(
                kv_ref.at[:, stored(firsts[part] + at, i), :],
                tiles.at[part, :, rows_at(at * per_block + i, SPAN), :],
                in_sem.at[part, at],
            ).start()

    def fetched(part, at):
        pltpu.make_async_copy(
            kv_ref.at[:, pl.ds(0, BLOCK), :], tiles.at[part, :, rows_at(at, BLOCK), :], in_sem.at[part, at]
        ).wait()

    def store(block):
        for i in range(per_block):
            pltpu.make_async_copy(
                sums.at[:, rows_at(block * per_block + i, SPAN), :],
                terms_ref.at[:, stored(block, i), :],
                out_sem.at[block],
            ).start()

    def stored_all(block):
        pltpu.make_async_copy(
            sums.at[:, rows_at(block, BLOCK), :], terms_ref.at[:, pl.ds(0, BLOCK), :], out_sem.at[block]
        ).wait()

    def shared(block):
        return (block >= firsts[1]) & (block <= lasts[1])

    for part in range(2):
        lax.fori_loop(0, lasts[part] - firsts[part] + 1, lambda at, c, part=part: (fetch(part, at), c)[1], 0)

    for part in range(2):
        base = bases[part]
        full_blocks = lasts[part] - firsts[part]
        inside = base - lasts[part] * BLOCK

        rows = pl.ds(part * SPAN, SPAN)
        q_rows = jnp.concatenate(
            [q_ref[rows, h * HD : (h + 1) * HD] for h in range(heads)], axis=0
        )
        g_rows = jnp.concatenate(
            [g_ref[rows, h * HD : (h + 1) * HD] for h in range(heads)], axis=0
        )
        q_t = as_f32(q_rows).T
        g_t = as_f32(g_rows).T
        q_cols[...] = q_t.astype(jnp.bfloat16)
        g_cols[...] = g_t.astype(jnp.bfloat16)

        def keys_at(at, size):
            return pl.ds(pl.multiple_of(at * BLOCK, BLOCK), size * BLOCK)

        def tile(which, at, size, part=part):
            return tiles[part, which, keys_at(at, size), :]

        def fold(value, op):
            value = value.reshape(value.shape[0] // 8, 8, cols)
            return op(value, axis=0)

        def score_step(at, size, top, part=part):
            for i in range(size):
                fetched(part, at + i)
            s = dot(tile(0, at, size), q_cols[...], (1, 0))
            scores[keys_at(at, size), :] = s
            return jnp.maximum(top, fold(s, jnp.max))

        top = over_blocks(full_blocks, score_step, jnp.full((8, cols), -1e30, jnp.float32))
        fetched(part, full_blocks)
        s = dot(tile(0, full_blocks, 1), q_cols[...], (1, 0))
        key_at = lax.broadcasted_iota(jnp.int32, (BLOCK, cols), 0)
        query_at = lax.broadcasted_iota(jnp.int32, (BLOCK, cols), 1)
        s = jnp.where(key_at <= inside + lax.rem(query_at, SPAN), s, -1e30)
        scores[keys_at(full_blocks, 1), :] = s
        top = jnp.max(jnp.maximum(top, fold(s, jnp.max)), axis=0, keepdims=True)

        acc[...] = jnp.zeros_like(acc)

        def value_step(at, size, total):
            p = jnp.exp2((scores[keys_at(at, size), :] - top) * to_exp2)
            p16 = p.astype(jnp.bfloat16)
            probs[keys_at(at, size), :] = p16
            acc[...] += dot(tile(1, at, size), p16, (0, 0))
            return total + fold(p, jnp.sum)

        total = over_blocks(full_blocks + 1, value_step, jnp.zeros((8, cols), jnp.float32))
        inverse = 1.0 / jnp.sum(total, axis=0, keepdims=True)
        out_t = (acc[...] * inverse).astype(jnp.bfloat16).astype(jnp.float32)
        delta = jnp.sum(g_t * out_t, axis=0, keepdims=True)
        q_scaled = (q_t * (inverse * scale)).astype(jnp.bfloat16)
        g_scaled = (g_t * inverse).astype(jnp.bfloat16)
        out_rows = out_t.T.astype(jnp.bfloat16)
        acc[...] = jnp.zeros_like(acc)

        def grad_step(at, size, carry, part=part):
            p16 = probs[keys_at(at, size), :]
            keys = tile(0, at, size)
            d_probs = dot(tile(1, at, size), g_cols[...], (1, 0))
            d_scores = (as_f32(p16) * (d_probs - delta)).astype(jnp.bfloat16)
            acc[...] += dot(keys, d_scores, (0, 0))
            d_key = dot(d_scores, q_scaled, (1, 1))
            d_value = dot(p16, g_scaled, (1, 1))
            for i in range(size):
                block = firsts[part] + at + i
                here = rows_at(block, BLOCK)
                for which, term in ((0, d_key), (1, d_value)):
                    term = term[i * BLOCK : (i + 1) * BLOCK]
                    if part > 0:
                        both = (block >= firsts[0]) & (block <= lasts[0])
                        term = term + jnp.where(both, as_f32(sums[which, here, :]), 0.0)
                    sums[which, here, :] = term.astype(jnp.bfloat16)
                if part > 0:
                    store(block)
                else:
                    pl.when(jnp.logical_not(shared(block)))(lambda block=block: store(block))
            return carry

        over_blocks(full_blocks + 1, grad_step, 0)
        dq_rows = (acc[...] * (inverse * scale)).T.astype(jnp.bfloat16)
        for h in range(heads):
            out_ref[rows, h * HD : (h + 1) * HD] = out_rows[h * SPAN : (h + 1) * SPAN]
            dq_ref[rows, h * HD : (h + 1) * HD] = dq_rows[h * SPAN : (h + 1) * SPAN]

    def drain(block, carry, part):
        if part > 0:
            stored_all(block)
        else:
            pl.when(jnp.logical_not(shared(block)))(lambda: stored_all(block))
        return carry

    for part in range(2):
        lax.fori_loop(firsts[part], lasts[part] + 1, lambda block, c, part=part: drain(block, c, part), 0)


def attention(doc_starts, assign, queries, d_out, kv_all, zeros):
    tokens = kv_all.shape[1]
    heads = queries.shape[1] // HD
    cols = heads * SPAN
    longest = tokens - (doc_starts.shape[0] - 1) * UNIT
    blocks = -(-longest // BLOCK)
    smem = pl.BlockSpec(memory_space=pltpu.SMEM)
    vmem = pl.BlockSpec(memory_space=pltpu.VMEM)
    anywhere = pl.BlockSpec(memory_space=pl.ANY)
    return pl.pallas_call(
        attention_kernel,
        out_shape=(
            jax.ShapeDtypeStruct(queries.shape, jnp.bfloat16),
            jax.ShapeDtypeStruct(queries.shape, jnp.bfloat16),
            jax.ShapeDtypeStruct(zeros.shape, jnp.bfloat16),
        ),
        in_specs=[smem, smem, vmem, vmem, anywhere, anywhere],
        out_specs=(vmem, vmem, anywhere),
        input_output_aliases={5: 2},
        scratch_shapes=[
            pltpu.SMEM(assign.shape, jnp.int32),
            pltpu.VMEM((2, 2, blocks * BLOCK, HD), jnp.bfloat16),
            pltpu.VMEM((2, tokens, HD), jnp.bfloat16),
            pltpu.VMEM((blocks * BLOCK, cols), jnp.float32),
            pltpu.VMEM((blocks * BLOCK, cols), jnp.bfloat16),
            pltpu.VMEM((HD, cols), jnp.bfloat16),
            pltpu.VMEM((HD, cols), jnp.bfloat16),
            pltpu.VMEM((HD, cols), jnp.float32),
            pltpu.SemaphoreType.DMA((2, blocks)),
            pltpu.SemaphoreType.DMA((tokens // BLOCK,)),
        ],
        compiler_params=pltpu.CompilerParams(vmem_limit_bytes=VMEM_BYTES),
    )(doc_starts, assign, queries, d_out, kv_all, zeros)


def body(queries, keys, values, d_out, doc_starts, assign):
    tokens = assign.shape[0] * SPAN
    dims = tuple(SIZES[axis] for axis in AXES)
    kv_all, zeros = gather_all(keys, values)
    attn_out, d_query, terms = attention(
        doc_starts, assign, queries, d_out, kv_all.reshape(2, tokens, HD), zeros.reshape(2, tokens, HD)
    )
    summed = reduce_all(terms.reshape(2, *dims, ROWS, HD))
    return (attn_out, d_query, summed[0], summed[1])


def solution(mesh):
    placed = (P("ctx", "head"), P("ctx", None), P("ctx", None), P("ctx", "head"), P(), P())
    return jax.shard_map(
        body,
        mesh=mesh,
        in_specs=placed,
        out_specs=(P("ctx", "head"), P("ctx", "head"), P("ctx", None), P("ctx", None)),
        check_vma=False,
    )
```

```python
import math

import jax
import jax.numpy as jnp
from jax import lax
from jax.experimental import pallas as pl
from jax.experimental.pallas import tpu as pltpu
from jax.sharding import PartitionSpec as P

HD = 128
SPAN = 64
ROWS = 2 * SPAN
BLOCK = 512
UNIT = 512
STEPS = (4, 2, 1)
MESH = pl.DeviceIdType.MESH
AXES = ("z", "y", "x")
SIZES = {"z": 8, "y": 4, "x": 4}
ROUTE_A = (0, 32)
ROUTES = ((32, 48, "y", "x"), (80, 48, "x", "y"))
NEAR = (1, -1, 2)
Z_AWAY = (1, -1, 2, -2, 3, -3, 4)
GROUPS = ((0,), (1, -1), (2, -2), (3, -3), (4,))
DIRECT = (4, 3, -3)
SUM_DIRECT = (0,)
COPIES = 74
ZERO_PIECES = 8
VMEM_BYTES = 60 * 1024 * 1024


def my_place():
    me = lax.axis_index("ctx")
    nx, ny = SIZES["x"], SIZES["y"]
    pos = {"x": lax.rem(me, nx), "y": lax.rem(me // nx, ny), "z": me // (nx * ny)}
    return pos, me, lax.axis_index("head")


def wrapped(value, size):
    return lax.rem(value + 2 * size, size)


def shifted(pos, axis, step):
    return wrapped(pos[axis] + step, SIZES[axis])


def peer(pos, core, axis, step):
    there = dict(pos)
    there[axis] = shifted(pos, axis, step)
    return ((there["z"] * SIZES["y"] + there["y"]) * SIZES["x"] + there["x"], core)


def greet(pos, me, core, along_z):
    barrier = pltpu.get_barrier_semaphore()
    partners = [("z", step) for step in along_z] + [(axis, step) for axis in "yx" for step in NEAR]
    for axis, step in partners:
        pl.semaphore_signal(
            barrier, inc=1, device_id=peer(pos, core, axis, step), device_id_type=MESH
        )
    pl.semaphore_signal(barrier, inc=1, device_id=(me, 1 - core), device_id_type=MESH)
    pl.semaphore_wait(barrier, len(partners) + 1)


def as_f32(value):
    return value.astype(jnp.float32)


class Numbers(dict):
    def __missing__(self, key):
        self[key] = len(self)
        assert len(self) <= COPIES
        return self[key]


def gather_kernel(
    k_ref, v_ref, all_ref, zeros_ref, recv, send_sem, side_send, side_recv, own_sem, zero_sem, blank
):
    pos, me, core = my_place()
    here = tuple(pl.ds(pos[axis], 1) for axis in AXES)
    for which, ref in ((0, k_ref), (1, v_ref)):
        @pl.when(core == which)
        def _(ref=ref):
            pltpu.make_async_copy(ref, all_ref.at[(core, *here)], own_sem).start()
    greet(pos, me, core, (1, -1))

    number = Numbers()
    sent_rows = []

    def view(owner, rows, **sel):
        index = [sel[axis] if axis in sel else (pos[axis], 1) for axis in AXES]
        return all_ref.at[(owner, *(pl.ds(*at) for at in index), pl.ds(*rows), slice(None))]

    def push(key, axis, step, rows, sel, src=None):
        ref = view(core, rows, **sel)
        pltpu.make_async_remote_copy(
            src_ref=ref if src is None else src.at[:, :, :, pl.ds(*rows), :],
            dst_ref=ref, send_sem=send_sem, recv_sem=recv.at[number[key]],
            device_id=peer(pos, core, axis, step), device_id_type=MESH,
        ).start()
        sent_rows.append(rows[1] * math.prod(count for _, count in sel.values()))

    def arrive(key, rows, sel):
        ref = view(core, rows, **sel)
        pltpu.make_async_remote_copy(
            src_ref=ref, dst_ref=ref, send_sem=send_sem, recv_sem=recv.at[number[key]],
            device_id=(me, 1 - core), device_id_type=MESH,
        ).wait_recv()

    def side(ref):
        return pltpu.make_async_remote_copy(
            src_ref=ref, dst_ref=ref, send_sem=side_send, recv_sem=side_recv,
            device_id=(me, 1 - core), device_id_type=MESH,
        )

    def hand_over(rows, **sel):
        side(view(core, rows, **sel)).start()

    def full(axis):
        return (0, SIZES[axis])

    def half(axis, side_at):
        return (side_at * (SIZES[axis] // 2), SIZES[axis] // 2)

    def z_way(route, d):
        if d == 4:
            return 1 - 2 * route
        return -1 if d > 0 else 1

    def at_z(d):
        return (shifted(pos, "z", d), 1)

    def to_z(route, d, src=None):
        first, count, _, _ = ROUTES[route]
        toward = z_way(route, d)
        push(("z", route, d), "z", toward, (first, count), {"z": at_z(d + toward)}, src)

    def from_z(route, d):
        first, count, _, _ = ROUTES[route]
        arrive(("z", route, d), (first, count), {"z": at_z(d)})
        if abs(d) < 3:
            to_z(route, d - z_way(route, d))
        elif d != 4 and z_way(route, d) == z_way(route, 4):
            to_z(route, 4)

    def to_middle(route, d, src=None):
        first, count, middle, _ = ROUTES[route]
        for m in NEAR:
            push(("m", route, d), middle, m, (first, count), {"z": at_z(d)}, src)

    def from_middle(route, d):
        first, count, middle, _ = ROUTES[route]
        arrive(("m", route, d), (first, count), {"z": at_z(d), middle: (0, len(NEAR))})

    def to_last(route, d):
        first, count, middle, last = ROUTES[route]
        sel = {"z": at_z(d), middle: full(middle)}
        for m in (NEAR if d in DIRECT else NEAR[:2]):
            push(("l", route, d), last, m, (first, count), sel)

    def whole_plane(route, d):
        first, count, _, _ = ROUTES[route]
        hand_over((first, count), z=at_z(d), y=full("y"), x=full("x"))

    def pass_last(route, d):
        first, count, middle, last = ROUTES[route]
        copies = len(NEAR) if d in DIRECT else 2
        arrive(("l", route, d), (first, count), {"z": at_z(d), middle: full(middle), last: (0, copies)})
        if d in DIRECT:
            whole_plane(route, d)
            return
        for way, m in enumerate(NEAR[:2]):
            sel = {"z": at_z(d), middle: half(middle, way), last: (shifted(pos, last, -m), 1)}
            push(("p", route, d), last, m, (first, count), sel)

    def from_last(route, d):
        first, count, middle, last = ROUTES[route]
        if d in DIRECT:
            return
        arrive(("p", route, d), (first, count), {"z": at_z(d), middle: full(middle)})
        whole_plane(route, d)

    def ring_sel(part, step, way, arriving):
        toward = 1 - 2 * way
        back = step if arriving else step - 1
        sel = {"z": (shifted(pos, "z", -toward * back), 1), "y": half("y", part), "x": full("x")}
        if step == SIZES["z"] // 2:
            sel["x"] = half("x", way)
        return sel

    def a_ring(step):
        steps = SIZES["z"] // 2
        for part in (0, 1):
            for way in (0, 1):
                if step > 1:
                    arrive(("r", part, step - 1, way), ROUTE_A, ring_sel(part, step - 1, way, True))
                if step <= steps:
                    push(("r", part, step, way), "z", 1 - 2 * way, ROUTE_A, ring_sel(part, step, way, False))
        for d in {1: (0,), steps + 1: (steps,)}.get(step, (step - 1, 1 - step)):
            hand_over(ROUTE_A, z=at_z(d), y=full("y"), x=full("x"))

    both = range(len(ROUTES))

    def begin(src):
        for route in both:
            for d in GROUPS[1]:
                to_z(route, d, src)
        for route in both:
            to_middle(route, 0, src)
        for m in NEAR:
            push(("y",), "y", m, ROUTE_A, {}, src)

    for which, ref in ((0, k_ref), (1, v_ref)):
        @pl.when(core == which)
        def _(ref=ref):
            sent_rows.clear()
            begin(ref)
    pltpu.make_async_copy(k_ref, all_ref.at[(core, *here)], own_sem).wait()
    blank[...] = jnp.zeros_like(blank)
    piece = blank.shape[0]
    pieces = zeros_ref.shape[0] // piece

    def wipe(at):
        return pltpu.make_async_copy(blank, zeros_ref.at[pl.ds(at * piece, piece)], zero_sem.at[at])

    for at in range(len(GROUPS) + 2):
        if at + 1 < len(GROUPS):
            for route in both:
                for d in GROUPS[at + 1]:
                    from_z(route, d)
                    to_middle(route, d)
        if at < len(GROUPS):
            for route in both:
                for d in GROUPS[at]:
                    from_middle(route, d)
                    to_last(route, d)
        if at == 0:
            arrive(("y",), ROUTE_A, {"y": (0, len(NEAR))})
            for m in NEAR:
                push(("x",), "x", m, ROUTE_A, {"y": full("y")})
        if at == 1:
            arrive(("x",), ROUTE_A, {"y": full("y"), "x": (0, len(NEAR))})
        if 0 < at <= SIZES["z"] // 2 + 1:
            a_ring(at)
        if 0 < at <= len(GROUPS):
            for route in both:
                for d in GROUPS[at - 1]:
                    pass_last(route, d)
        if 1 < at:
            for route in both:
                for d in GROUPS[at - 2]:
                    from_last(route, d)
        for i in range(at * 2, min(at * 2 + 2, pieces)):
            wipe(i).start()
    for at in range(pieces):
        wipe(at).wait()
    sent = zeros_ref.at[pl.ds(0, sum(sent_rows))]
    pltpu.make_async_remote_copy(
        src_ref=sent, dst_ref=sent, send_sem=send_sem, recv_sem=side_recv,
        device_id=(me, 1 - core), device_id_type=MESH,
    ).wait_send()
    side(all_ref.at[core]).wait_send()
    side(all_ref.at[1 - core]).wait_recv()


def gather_all(keys, values):
    dims = tuple(SIZES[axis] for axis in AXES)
    sems = pltpu.SemaphoreType.DMA((COPIES,))
    one_sem = pltpu.SemaphoreType.DMA
    piece = 2 * math.prod(dims) * ROWS // ZERO_PIECES
    anywhere = pl.BlockSpec(memory_space=pl.ANY)
    return pl.pallas_call(
        gather_kernel,
        out_shape=(
            jax.ShapeDtypeStruct((2, *dims, ROWS, HD), jnp.bfloat16),
            jax.ShapeDtypeStruct((ZERO_PIECES * piece, HD), jnp.bfloat16),
        ),
        in_specs=[anywhere, anywhere],
        out_specs=(anywhere, anywhere),
        scratch_shapes=[sems, one_sem, one_sem, one_sem, one_sem,
                        pltpu.SemaphoreType.DMA((ZERO_PIECES,)), pltpu.VMEM((piece, HD), jnp.bfloat16)],
        compiler_params=pltpu.CompilerParams(
            collective_id=0, has_side_effects=True, vmem_limit_bytes=VMEM_BYTES
        ),
    )(keys.reshape(1, 1, 1, ROWS, HD), values.reshape(1, 1, 1, ROWS, HD))


def reduce_kernel(
    terms_ref, out_ref, held, other, final, ring_land, ax_land, ay_land, first_land, second_land,
    direct_land, middle_land, z_land, send, recv, load_sem, side_send, side_recv, last_send, last_recv,
):
    pos, me, core = my_place()
    sibling = (me, 1 - core)

    def load(d):
        z = shifted(pos, "z", d)
        return pltpu.make_async_copy(terms_ref.at[core, z], held.at[z], load_sem.at[d % 8])

    def side(d):
        z = shifted(pos, "z", d)
        return pltpu.make_async_remote_copy(
            src_ref=terms_ref.at[1 - core, z], dst_ref=other.at[z],
            send_sem=side_send, recv_sem=side_recv.at[d % 8],
            device_id=sibling, device_id_type=MESH,
        )

    far_first = GROUPS[::-1]
    for group in far_first:
        for d in group:
            load(d).start()
    greet(pos, me, core, Z_AWAY)
    for group in far_first:
        for d in group:
            side(d).start()

    number, kind = Numbers(), Numbers()

    def copy(key, axis, step, src, dst):
        return pltpu.make_async_remote_copy(
            src_ref=src, dst_ref=dst, send_sem=send.at[kind[key[0]]], recv_sem=recv.at[number[key]],
            device_id=peer(pos, core, axis, step), device_id_type=MESH,
        )

    def push(*item):
        copy(*item).start()

    def arrived(key, land):
        copy(key, "z", 1, land, land).wait_recv()

    def left(name, land):
        copy((name,), "z", 1, land, land).wait_send()

    def held_at(rows, **sel):
        index = []
        for axis in AXES:
            at = sel[axis] if axis in sel else pos[axis]
            index.append(pl.ds(*at) if isinstance(at, tuple) else at)
        return (*index, pl.ds(*rows), slice(None))

    def add(where, lands):
        total = as_f32(held[where])
        for land in lands:
            total = total + as_f32(land[...])
        held[where] = total.astype(jnp.bfloat16)

    def join(d):
        load(d).wait()
        side(d).wait_recv()
        z = shifted(pos, "z", d)

        def one(y, carry):
            for x in range(SIZES["x"]):
                held[z, y, x] = (as_f32(held[z, y, x]) + as_f32(other[z, y, x])).astype(jnp.bfloat16)
            return carry

        lax.fori_loop(0, SIZES["y"], one, 0)

    def middle_half(middle, way):
        size = SIZES[middle] // 2
        return (way * size, size)

    def first_copy(route, d, way):
        first, count, middle, last = ROUTES[route]
        where = {"z": shifted(pos, "z", d), middle: middle_half(middle, way), last: shifted(pos, last, 2)}
        return (("f", route, d), last, 1 - 2 * way, held.at[held_at((first, count), **where)],
                first_land.at[route, d % 8, way])

    def second_copy(route, d, way):
        first, count, middle, last = ROUTES[route]
        where = {"z": shifted(pos, "z", d), middle: (0, SIZES[middle]), last: shifted(pos, last, 1 - 2 * way)}
        return (("s", route, d), last, 1 - 2 * way, held.at[held_at((first, count), **where)],
                second_land.at[route, d % 8, way])

    def middle_copy(route, d, m):
        first, count, middle, last = ROUTES[route]
        where = {"z": shifted(pos, "z", d), middle: shifted(pos, middle, m)}
        return (("m", route, d), middle, m, held.at[held_at((first, count), **where)],
                middle_land.at[route, d % 8, NEAR.index(m)])

    def z_copy(route, d):
        first, count, _, _ = ROUTES[route]
        return (("z", route), "z", d, held.at[held_at((first, count), z=shifted(pos, "z", d))],
                z_land.at[route, Z_AWAY.index(d)])

    def direct_copy(route, d, m):
        first, count, middle, last = ROUTES[route]
        where = {"z": shifted(pos, "z", d), middle: (0, SIZES[middle]), last: shifted(pos, last, m)}
        return (("d", route, d), last, m, held.at[held_at((first, count), **where)],
                direct_land.at[route, SUM_DIRECT.index(d), NEAR.index(m)])

    def send_first(route, d):
        if d in SUM_DIRECT:
            for m in NEAR:
                push(*direct_copy(route, d, m))
            return
        for way in (0, 1):
            push(*first_copy(route, d, way))

    def send_second(route, d):
        first, count, middle, last = ROUTES[route]
        arrived(("f", route, d), first_land.at[route, d % 8])
        for way in (0, 1):
            low, size = middle_half(middle, way)
            for i in range(size):
                where = {"z": shifted(pos, "z", d), middle: low + i, last: shifted(pos, last, 1 - 2 * way)}
                add(held_at((first, count), **where), [first_land.at[route, d % 8, way, i]])
            push(*second_copy(route, d, way))

    def send_middle(route, d):
        first, count, middle, last = ROUTES[route]
        if d in SUM_DIRECT:
            arrived(("d", route, d), direct_land.at[route, SUM_DIRECT.index(d)])
            lands = [direct_land.at[route, SUM_DIRECT.index(d), i] for i in range(len(NEAR))]
        else:
            arrived(("s", route, d), second_land.at[route, d % 8])
            lands = [second_land.at[route, d % 8, way] for way in (0, 1)]
        for i in range(SIZES[middle]):
            where = {"z": shifted(pos, "z", d), middle: i}
            add(held_at((first, count), **where), [land.at[i] for land in lands])
        for m in NEAR:
            push(*middle_copy(route, d, m))

    def send_z(route, d):
        first, count, _, _ = ROUTES[route]
        arrived(("m", route, d), middle_land.at[route, d % 8])
        where = held_at((first, count), z=shifted(pos, "z", d))
        add(where, [middle_land.at[route, d % 8, i] for i in range(len(NEAR))])
        if d != 0:
            push(*z_copy(route, d))

    def ring_copy(step, way):
        toward = 1 - 2 * way
        half = SIZES["x"] // 2
        xs = (way * half, half) if step == 1 else (0, SIZES["x"])
        where = {"z": shifted(pos, "z", toward * (5 - step)), "y": (0, SIZES["y"]), "x": xs}
        return (("h" if step == 1 else "r", step, way), "z", toward, held.at[held_at(ROUTE_A, **where)],
                ring_land.at[way, step - 1, :, pl.ds(*xs)])

    def ring(step):
        for way in (0, 1):
            toward = 1 - 2 * way
            half = SIZES["x"] // 2
            if 1 < step < 5:
                copy(*ring_copy(step - 1, way)).wait_recv()
                low, size = (way * half, half) if step == 2 else (0, SIZES["x"])
                z = shifted(pos, "z", toward * (5 - step))

                def one(y, carry):
                    for i in range(size):
                        add(held_at(ROUTE_A, z=z, y=y, x=low + i), [ring_land.at[way, step - 2, y, low + i]])
                    return carry

                lax.fori_loop(0, SIZES["y"], one, 0)
            if step < 5:
                push(*ring_copy(step, way))
        if step == 5:
            for way in (0, 1):
                copy(*ring_copy(4, way)).wait_recv()

            def last(y, carry):
                for x in range(SIZES["x"]):
                    add(held_at(ROUTE_A, y=y, x=x), [ring_land.at[way, 3, y, x] for way in (0, 1)])
                return carry

            lax.fori_loop(0, SIZES["y"], last, 0)

    def ax_copy(m):
        where = {"y": (0, SIZES["y"]), "x": shifted(pos, "x", m)}
        return (("ax",), "x", m, held.at[held_at(ROUTE_A, **where)], ax_land.at[NEAR.index(m)])

    def ay_copy(m):
        where = {"y": shifted(pos, "y", m)}
        return (("ay",), "y", m, held.at[held_at(ROUTE_A, **where)], ay_land.at[NEAR.index(m)])

    both = range(len(ROUTES))
    for at in range(len(far_first) + 2):
        if at < len(far_first):
            for d in far_first[at]:
                join(d)
            for route in both:
                for d in far_first[at]:
                    send_first(route, d)
        for behind, act in ((1, send_second), (2, send_middle), (3, send_z)):
            for begun, group in enumerate(far_first):
                for d in group:
                    sooner = 1 if d in SUM_DIRECT else 0
                    if begun + behind - sooner == at and not (sooner and act is send_second):
                        for route in both:
                            act(route, d)
        if at < len(far_first):
            ring(at + 1)
        if at == len(far_first) - 1:
            for m in NEAR:
                push(*ax_copy(m))
        if at == len(far_first):
            arrived(("ax",), ax_land)
            for y in range(SIZES["y"]):
                add(held_at(ROUTE_A, y=y), [ax_land.at[i, y] for i in range(len(NEAR))])
            for m in NEAR:
                push(*ay_copy(m))
    arrived(("ay",), ay_land)
    add(held_at(ROUTE_A), [ay_land.at[i] for i in range(len(NEAR))])
    for route in both:
        first, count, _, _ = ROUTES[route]
        arrived(("z", route), z_land.at[route])
        add(held_at((first, count)), [z_land.at[route, i] for i in range(len(Z_AWAY))])

    final[core] = held[pos["z"], pos["y"], pos["x"]]
    last_copy = pltpu.make_async_remote_copy(
        src_ref=final.at[core], dst_ref=final.at[core], send_sem=last_send, recv_sem=last_recv,
        device_id=sibling, device_id_type=MESH,
    )
    last_copy.start()
    pltpu.make_async_remote_copy(
        src_ref=other, dst_ref=other, send_sem=side_send, recv_sem=last_recv,
        device_id=sibling, device_id_type=MESH,
    ).wait_send()
    relayed = pl.ds(0, SIZES["z"] - len(SUM_DIRECT))
    left("f", first_land.at[:, relayed])
    left("s", second_land.at[:, relayed])
    left("d", direct_land)
    left("m", middle_land)
    left("z", z_land)
    left("h", ring_land.at[:, 0, :, pl.ds(0, SIZES["x"] // 2)])
    left("r", ring_land.at[:, pl.ds(1, 3)])
    left("ax", ax_land)
    left("ay", ay_land)
    last_copy.wait()
    out_ref[...] = final[...]


def reduce_all(terms):
    dims = tuple(SIZES[axis] for axis in AXES)
    nz, ny, nx = dims

    def vmem(*shape):
        return pltpu.VMEM((*shape, HD), jnp.bfloat16)

    count = ROUTES[0][1]
    routes = len(ROUTES)
    sems = pltpu.SemaphoreType.DMA((COPIES,))
    by_z = pltpu.SemaphoreType.DMA((nz,))
    one_sem = pltpu.SemaphoreType.DMA
    return pl.pallas_call(
        reduce_kernel,
        out_shape=jax.ShapeDtypeStruct((2, ROWS, HD), jnp.bfloat16),
        in_specs=[pl.BlockSpec(memory_space=pl.ANY)],
        out_specs=pl.BlockSpec(memory_space=pltpu.VMEM),
        scratch_shapes=[
            vmem(*dims, ROWS),
            vmem(*dims, ROWS),
            vmem(2, ROWS),
            vmem(2, nz // 2, ny, nx, ROUTE_A[1]),
            vmem(len(NEAR), ny, ROUTE_A[1]),
            vmem(len(NEAR), ROUTE_A[1]),
            vmem(routes, nz, 2, 2, count),
            vmem(routes, nz, 2, 4, count),
            vmem(routes, len(SUM_DIRECT), len(NEAR), 4, count),
            vmem(routes, nz, len(NEAR), count),
            vmem(routes, len(Z_AWAY), count),
            pltpu.SemaphoreType.DMA((9,)), sems, by_z, one_sem, by_z, one_sem, one_sem,
        ],
        compiler_params=pltpu.CompilerParams(
            collective_id=1, has_side_effects=True, vmem_limit_bytes=VMEM_BYTES
        ),
    )(terms)


def dot(left, right, contract):
    return lax.dot_general(
        left, right, ((contract[:1], contract[1:]), ((), ())), preferred_element_type=jnp.float32
    )


def over_blocks(count, step, carry):
    done = jnp.int32(0)
    for size in STEPS:
        steps = (count - done) // size
        carry = lax.fori_loop(
            0, steps, lambda at, c, done=done, size=size: step(done + at * size, size, c), carry
        )
        done = done + steps * size
    return carry


def attention_kernel(
    starts_ref, assign_ref, q_ref, g_ref, kv_ref, zeros_ref, out_ref, dq_ref, terms_ref,
    place_ref, tiles, sums, scores, probs, q_cols, g_cols, acc, in_sem, out_sem,
):
    del zeros_ref
    heads = q_ref.shape[1] // HD
    cols = heads * SPAN
    scale = 1.0 / math.sqrt(HD)
    to_exp2 = scale * math.log2(math.e)
    per_block = BLOCK // SPAN

    def locate(at, carry):
        for i in range(16):
            place_ref[assign_ref[at * 16 + i]] = at * 16 + i
        return carry

    lax.fori_loop(0, assign_ref.shape[0] // 16, locate, 0)
    first_span = lax.axis_index("ctx") * 2
    bases, firsts, lasts = [], [], []
    for part in range(2):
        base = assign_ref[first_span + part] * SPAN
        doc_first = jnp.int32(0)
        for doc in range(starts_ref.shape[0]):
            start = starts_ref[doc]
            doc_first = jnp.where(start <= base, jnp.maximum(doc_first, start), doc_first)
        bases.append(base)
        firsts.append(doc_first // BLOCK)
        lasts.append(base // BLOCK)

    def rows_at(at, count):
        return pl.ds(pl.multiple_of(at * count, count), count)

    def stored(block, i):
        return rows_at(place_ref[block * per_block + i], SPAN)

    def fetch(part, at):
        for i in range(per_block):
            pltpu.make_async_copy(
                kv_ref.at[:, stored(firsts[part] + at, i), :],
                tiles.at[part, :, rows_at(at * per_block + i, SPAN), :],
                in_sem.at[part, at],
            ).start()

    def fetched(part, at):
        pltpu.make_async_copy(
            kv_ref.at[:, pl.ds(0, BLOCK), :], tiles.at[part, :, rows_at(at, BLOCK), :], in_sem.at[part, at]
        ).wait()

    def store(block):
        for i in range(per_block):
            pltpu.make_async_copy(
                sums.at[:, rows_at(block * per_block + i, SPAN), :],
                terms_ref.at[:, stored(block, i), :],
                out_sem.at[block],
            ).start()

    def stored_all(block):
        pltpu.make_async_copy(
            sums.at[:, rows_at(block, BLOCK), :], terms_ref.at[:, pl.ds(0, BLOCK), :], out_sem.at[block]
        ).wait()

    def shared(block):
        return (block >= firsts[1]) & (block <= lasts[1])

    for part in range(2):
        lax.fori_loop(0, lasts[part] - firsts[part] + 1, lambda at, c, part=part: (fetch(part, at), c)[1], 0)

    for part in range(2):
        rows = pl.ds(part * SPAN, SPAN)
        for ref, turned in ((q_ref, q_cols), (g_ref, g_cols)):
            stacked = jnp.concatenate(
                [ref[rows, h * HD : (h + 1) * HD] for h in range(heads)], axis=0
            )
            turned[part] = as_f32(stacked).T.astype(jnp.bfloat16)

    for part in range(2):
        base = bases[part]
        full_blocks = lasts[part] - firsts[part]
        inside = base - lasts[part] * BLOCK

        rows = pl.ds(part * SPAN, SPAN)

        def keys_at(at, size):
            return pl.ds(pl.multiple_of(at * BLOCK, BLOCK), size * BLOCK)

        def tile(which, at, size, part=part):
            return tiles[part, which, keys_at(at, size), :]

        def fold(value, op):
            value = value.reshape(value.shape[0] // 8, 8, cols)
            return op(value, axis=0)

        def score_step(at, size, top, part=part):
            for i in range(size):
                fetched(part, at + i)
            s = dot(tile(0, at, size), q_cols[part], (1, 0))
            scores[keys_at(at, size), :] = s
            return jnp.maximum(top, fold(s, jnp.max))

        top = over_blocks(full_blocks, score_step, jnp.full((8, cols), -1e30, jnp.float32))
        fetched(part, full_blocks)
        s = dot(tile(0, full_blocks, 1), q_cols[part], (1, 0))
        key_at = lax.broadcasted_iota(jnp.int32, (BLOCK, cols), 0)
        query_at = lax.broadcasted_iota(jnp.int32, (BLOCK, cols), 1)
        s = jnp.where(key_at <= inside + lax.rem(query_at, SPAN), s, -1e30)
        scores[keys_at(full_blocks, 1), :] = s
        top = jnp.max(jnp.maximum(top, fold(s, jnp.max)), axis=0, keepdims=True)

        acc[...] = jnp.zeros_like(acc)

        def value_step(at, size, total):
            p = jnp.exp2((scores[keys_at(at, size), :] - top) * to_exp2)
            p16 = p.astype(jnp.bfloat16)
            probs[keys_at(at, size), :] = p16
            acc[...] += dot(tile(1, at, size), p16, (0, 0))
            return total + fold(p, jnp.sum)

        total = over_blocks(full_blocks + 1, value_step, jnp.zeros((8, cols), jnp.float32))
        inverse = 1.0 / jnp.sum(total, axis=0, keepdims=True)
        out_t = (acc[...] * inverse).astype(jnp.bfloat16).astype(jnp.float32)
        delta = jnp.sum(as_f32(g_cols[part]) * out_t, axis=0, keepdims=True)
        q_scaled = (as_f32(q_cols[part]) * (inverse * scale)).astype(jnp.bfloat16)
        g_scaled = (as_f32(g_cols[part]) * inverse).astype(jnp.bfloat16)
        out_rows = out_t.T.astype(jnp.bfloat16)
        acc[...] = jnp.zeros_like(acc)

        def grad_step(at, size, carry, part=part):
            p16 = probs[keys_at(at, size), :]
            keys = tile(0, at, size)
            d_probs = dot(tile(1, at, size), g_cols[part], (1, 0))
            d_scores = (as_f32(p16) * (d_probs - delta)).astype(jnp.bfloat16)
            acc[...] += dot(keys, d_scores, (0, 0))
            d_key = dot(d_scores, q_scaled, (1, 1))
            d_value = dot(p16, g_scaled, (1, 1))
            for i in range(size):
                block = firsts[part] + at + i
                here = rows_at(block, BLOCK)
                for which, term in ((0, d_key), (1, d_value)):
                    term = term[i * BLOCK : (i + 1) * BLOCK]
                    if part > 0:
                        both = (block >= firsts[0]) & (block <= lasts[0])
                        term = term + jnp.where(both, as_f32(sums[which, here, :]), 0.0)
                    sums[which, here, :] = term.astype(jnp.bfloat16)
                if part > 0:
                    store(block)
                else:
                    pl.when(jnp.logical_not(shared(block)))(lambda block=block: store(block))
            return carry

        over_blocks(full_blocks + 1, grad_step, 0)
        dq_rows = (acc[...] * (inverse * scale)).T.astype(jnp.bfloat16)
        for h in range(heads):
            out_ref[rows, h * HD : (h + 1) * HD] = out_rows[h * SPAN : (h + 1) * SPAN]
            dq_ref[rows, h * HD : (h + 1) * HD] = dq_rows[h * SPAN : (h + 1) * SPAN]

    def drain(block, carry, part):
        if part > 0:
            stored_all(block)
        else:
            pl.when(jnp.logical_not(shared(block)))(lambda: stored_all(block))
        return carry

    for part in range(2):
        lax.fori_loop(firsts[part], lasts[part] + 1, lambda block, c, part=part: drain(block, c, part), 0)


def attention(doc_starts, assign, queries, d_out, kv_all, zeros):
    tokens = kv_all.shape[1]
    heads = queries.shape[1] // HD
    cols = heads * SPAN
    longest = tokens - (doc_starts.shape[0] - 1) * UNIT
    blocks = -(-longest // BLOCK)
    smem = pl.BlockSpec(memory_space=pltpu.SMEM)
    vmem = pl.BlockSpec(memory_space=pltpu.VMEM)
    anywhere = pl.BlockSpec(memory_space=pl.ANY)
    return pl.pallas_call(
        attention_kernel,
        out_shape=(
            jax.ShapeDtypeStruct(queries.shape, jnp.bfloat16),
            jax.ShapeDtypeStruct(queries.shape, jnp.bfloat16),
            jax.ShapeDtypeStruct(zeros.shape, jnp.bfloat16),
        ),
        in_specs=[smem, smem, vmem, vmem, anywhere, anywhere],
        out_specs=(vmem, vmem, anywhere),
        input_output_aliases={5: 2},
        scratch_shapes=[
            pltpu.SMEM(assign.shape, jnp.int32),
            pltpu.VMEM((2, 2, blocks * BLOCK, HD), jnp.bfloat16),
            pltpu.VMEM((2, tokens, HD), jnp.bfloat16),
            pltpu.VMEM((blocks * BLOCK, cols), jnp.float32),
            pltpu.VMEM((blocks * BLOCK, cols), jnp.bfloat16),
            pltpu.VMEM((2, HD, cols), jnp.bfloat16),
            pltpu.VMEM((2, HD, cols), jnp.bfloat16),
            pltpu.VMEM((HD, cols), jnp.float32),
            pltpu.SemaphoreType.DMA((2, blocks)),
            pltpu.SemaphoreType.DMA((tokens // BLOCK,)),
        ],
        compiler_params=pltpu.CompilerParams(vmem_limit_bytes=VMEM_BYTES),
    )(doc_starts, assign, queries, d_out, kv_all, zeros)


def body(queries, keys, values, d_out, doc_starts, assign):
    tokens = assign.shape[0] * SPAN
    dims = tuple(SIZES[axis] for axis in AXES)
    kv_all, zeros = gather_all(keys, values)
    attn_out, d_query, terms = attention(
        doc_starts, assign, queries, d_out, kv_all.reshape(2, tokens, HD), zeros.reshape(2, tokens, HD)
    )
    summed = reduce_all(terms.reshape(2, *dims, ROWS, HD))
    return (attn_out, d_query, summed[0], summed[1])


def solution(mesh):
    placed = (P("ctx", "head"), P("ctx", None), P("ctx", None), P("ctx", "head"), P(), P())
    return jax.shard_map(
        body,
        mesh=mesh,
        in_specs=placed,
        out_specs=(P("ctx", "head"), P("ctx", "head"), P("ctx", None), P("ctx", None)),
        check_vma=False,
    )
```
